512 devices in a mesh: gx: 16 (over y, core), gy: 32 (over z, x).
Axes of the slice: x: 4, y: 8, z: 8, core: 2. Of those that a mesh axis runs over, the one named last changes fastest.
Arguments:
- concentration: float32 [2048, 4, 4, 4096], P('gx', None, None, 'gy'), may hold values from -6 to 6
- courant_x: float32 [2048, 4, 4096], P('gx', None, 'gy'), may hold values from 300 to 1200
- courant_y: float32 [2048, 4, 4096], P('gx', None, 'gy'), may hold values from -0.4 to 0.4
- vert_diff: float32 [2048, 4, 4096], P('gx', None, 'gy'), may hold values from 0.05 to 0.45
- emission: float32 [2048, 4, 4096], P('gx', None, 'gy'), may hold values from -6 to 6
- building: int32 [16, 32], P('gx', 'gy'), may hold values 0 or 1
Outputs:
- updated: float32 [2048, 4, 4, 4096], P('gx', None, None, 'gy')
The draws below stay inside these ranges and needn't reach their ends.
Inputs may be any that keep to these rules, and one draw needn't show every extreme that they name: 1 marks a tile filled by a building, 0 a fluid tile.
All inputs are finite; a program needn't handle non-finite values. No bound on the sum of `building` on one device may be relied on, other than what follows from the above.
Results may differ from the reference program's by a relative error of at most 0.00002.
Values sent between devices are 32-bit elements; how exact they have to be, the bound alone decides.
No kernel may reach another device: no remote copies, remote signals or barrier semaphores. Data moves between devices by JAX's collectives and lax.ppermute only.
A program may use at most 64 MiB of HBM per device.

```python
import math
import jax
import jax.numpy as jnp
from jax import lax

NT = 4
NL = 4
TILE = 128
NX = 2048
NY = 4096


def touch_ends(entries, rng, low, top_value):
    spot = [jax.random.randint(jax.random.fold_in(rng, axis), (), 0, length) for axis, length in enumerate(entries.shape)]
    widest = entries.shape.index(max(entries.shape))
    neighbour = spot[:widest] + [(spot[widest] + 1) % entries.shape[widest]] + spot[widest + 1:]
    return entries.at[tuple(spot)].set(low).at[tuple(neighbour)].set(top_value)


def shard_levels(own_key, shape, cuts, least, top_value):
    def one(position, blocks):
        steps = jax.random.uniform(jax.random.fold_in(jax.random.fold_in(own_key, 6), position), (blocks,), jnp.float32, least / len(cuts), top_value / len(cuts))
        return jnp.repeat(jnp.exp(steps), shape[position] // blocks).reshape((-1,) + (1,) * (len(shape) - position - 1))

    level = one(*cuts[0])
    for cut in cuts[1:]:
        level = level * one(*cut)
    return level


def centred(own_key, shape, deviation, bound, shards=(), held_as=jnp.bfloat16):
    loudness = shard_levels(own_key, shape, shards, -0.22, 0.18) if shards else 1.0
    entries = jax.random.normal(own_key, shape, jnp.float32) * deviation * loudness
    return jnp.minimum(jnp.maximum(entries, -bound), bound).astype(held_as)


def setup_inputs(seed: int = 0) -> dict:
    seeds = jax.random.split(jax.random.key(seed), 7)
    concentration = centred(seeds[0], (NX, NT, NL, NY), 1.0, 6.0, ((0, 16), (3, 32)), jnp.float32)
    courant_x = jnp.clip(jnp.exp(math.log(1200.0) - 1.3862944 * jax.random.uniform(seeds[1], (NX, NL, NY), jnp.float32) ** shard_levels(seeds[1], (NX, NL, NY), ((0, 16), (2, 32)), -0.2, 0.2)), 300.0, 1200.0)
    courant_y = jnp.clip(jax.random.uniform(seeds[2], (NX, NL, NY), jnp.float32, -0.4, 0.4) * shard_levels(seeds[2], (NX, NL, NY), ((0, 16), (2, 32)), -0.4, 0.0), -0.4, 0.4)
    vert_diff = jnp.clip(jnp.exp(math.log(0.45) - 2.1972245 * jax.random.uniform(seeds[3], (NX, NL, NY), jnp.float32) ** shard_levels(seeds[3], (NX, NL, NY), ((0, 16), (2, 32)), -0.2, 0.2)), 0.05, 0.45)
    emission = centred(seeds[4], (NX, NT, NY), 1.0, 6.0, ((0, 16), (2, 32)), jnp.float32)
    building = touch_ends((jax.random.randint(seeds[5], (NX // TILE, NY // TILE), 0, 3) < 1).astype(jnp.int32), jax.random.fold_in(seeds[5], 1), 0, 1)
    return {"concentration": concentration, "courant_x": courant_x, "courant_y": courant_y, "vert_diff": vert_diff, "emission": emission, "building": building}


cross_diff = 300.0
span_diff = 0.25


def spanwise(tracer_field, span_courant):
    left_cells = jnp.roll(tracer_field, 1, axis=3)
    right_cells = jnp.roll(tracer_field, -1, axis=3)
    wind_pos = jnp.maximum(span_courant, 0.0)[:, None]
    wind_neg = jnp.maximum(-span_courant, 0.0)[:, None]
    return wind_pos * (left_cells - tracer_field) + wind_neg * (right_cells - tracer_field) + span_diff * (left_cells + right_cells - 2.0 * tracer_field)


def vertical(tracer_field, face_diff):
    upper_diff = jnp.concatenate([face_diff[:, 1:], jnp.zeros_like(face_diff[:, :1])], axis=1)[:, None]
    lower_diff = face_diff[:, None]
    below_cells = jnp.concatenate([jnp.zeros_like(tracer_field[:, :, :1]), tracer_field[:, :, :-1]], axis=2)
    above_cells = jnp.concatenate([tracer_field[:, :, 1:], jnp.zeros_like(tracer_field[:, :, :1])], axis=2)
    return lower_diff * (below_cells - tracer_field) + upper_diff * (above_cells - tracer_field)


def vertical_solve(forcing, face_diff):
    level_total = forcing.shape[2]
    factors = []
    partials = []
    prev_factor = None
    prev_partial = None
    for level_index in range(level_total):
        below_diff = face_diff[:, level_index]
        if level_index + 1 < level_total:
            above_diff = face_diff[:, level_index + 1]
        else:
            above_diff = jnp.zeros_like(below_diff)
        diagonal = 1.0 + below_diff + above_diff
        if level_index == 0:
            pivots = diagonal
            partial_value = forcing[:, :, 0] / pivots[:, None]
        else:
            pivots = diagonal + below_diff * prev_factor
            partial_value = (forcing[:, :, level_index] + below_diff[:, None] * prev_partial) / pivots[:, None]
        prev_factor = -above_diff / pivots
        prev_partial = partial_value
        factors.append(prev_factor)
        partials.append(partial_value)
    results = [None] * level_total
    results[level_total - 1] = partials[level_total - 1]
    for level_index in range(level_total - 2, -1, -1):
        results[level_index] = partials[level_index] - factors[level_index][:, None] * results[level_index + 1]
    return jnp.stack(results, axis=2)


def streamwise_solve(lower_coef, diag_coef, upper_coef, forcing):
    def forward(carried, inputs):
        prev_factor, prev_partial = carried
        low_row, diag_row, up_row, force_row = inputs
        pivots = diag_row - low_row * prev_factor
        factor = up_row / pivots
        partial_row = (force_row - low_row[None] * prev_partial) / pivots[None]
        return (factor, partial_row), (factor, partial_row)

    start_state = (jnp.zeros(diag_coef.shape[1:], diag_coef.dtype), jnp.zeros(forcing.shape[1:], forcing.dtype))
    final_state, stacked = lax.scan(forward, start_state, (lower_coef, diag_coef, upper_coef, forcing))

    def backward(carried, inputs):
        factor, partial_row = inputs
        solved_row = partial_row - factor[None] * carried
        return solved_row, solved_row

    last_state, solution = lax.scan(backward, jnp.zeros(forcing.shape[1:], forcing.dtype), stacked, reverse=True)
    return solution


def reference(concentration, courant_x, courant_y, vert_diff, emission, building):
    solid_map = jnp.repeat(jnp.repeat(building, TILE, axis=0), TILE, axis=1)
    fluid_map = 1.0 - solid_map.astype(jnp.float32)
    fluid_cells = fluid_map[:, None, :]
    fluid_field = fluid_map[:, None, None, :]
    base_side = concentration + spanwise(concentration, courant_y) + vertical(concentration, vert_diff)
    base_side = base_side.at[:, :, 0].add(emission)
    first_side = fluid_field * base_side
    lower_coef = -fluid_cells * (courant_x + cross_diff)
    diag_coef = 1.0 + fluid_cells * (courant_x + 2.0 * cross_diff)
    upper_coef = -fluid_cells * cross_diff * jnp.ones_like(courant_x)
    star = streamwise_solve(lower_coef, diag_coef, upper_coef, first_side)
    second_side = fluid_field * (2.0 * star - first_side + spanwise(star, courant_y))
    return vertical_solve(second_side, vert_diff)
```

```python
import functools

import jax
import jax.numpy as jnp
from jax import lax
from jax.experimental import pallas as pl
from jax.experimental.pallas import tpu as pltpu
from jax.sharding import PartitionSpec as P

cross_diff = 300.0
span_diff = 0.25

SUB, LANE = 8, 128
VMEM = pl.BlockSpec(memory_space=pltpu.VMEM)
SMEM = pl.BlockSpec(memory_space=pltpu.SMEM)
LIMIT = 16 * 1024 * 1024


def sub_ids():
    return lax.broadcasted_iota(jnp.int32, (SUB, LANE), 0)


def lane_ids():
    return lax.broadcasted_iota(jnp.int32, (SUB, LANE), 1)


def lanes(x, shift):
    shift %= LANE
    return pltpu.roll(x, shift, 1) if shift else x


def subs(x, shift):
    shift %= SUB
    return pltpu.roll(x, shift, 0) if shift else x


def fluid_of(building_ref):
    return 1.0 - building_ref[0, 0].astype(jnp.float32)


def both_rows(pair):
    low = sub_ids() < 4
    turned = subs(pair, 4)
    return jnp.where(low, pair, turned), jnp.where(low, turned, pair)


def level_above(x):
    return jnp.where(sub_ids() % 4 == 3, 0.0, subs(x, -1))


def level_below(x):
    return jnp.where(sub_ids() % 4 == 0, 0.0, subs(x, 1))


def span_operator(q, left, right, wind):
    wind_pos = jnp.maximum(wind, 0.0)
    wind_neg = jnp.maximum(-wind, 0.0)
    return (wind_pos + span_diff) * (left - q) + (wind_neg + span_diff) * (right - q)


def side_of(q, left, right, wind, face, face_up, source, fluid):
    value = q + span_operator(q, left, right, wind)
    value = value + face * (level_below(q) - q) + face_up * (level_above(q) - q)
    return fluid * (value + source)


def pack_kernel(c_ref, cx_ref, cy_ref, vd_ref, em_ref, building_ref, a_ref, b_ref):
    lane, sub = lane_ids(), sub_ids()
    fluid = fluid_of(building_ref)
    low = sub < 4
    even_gy = lax.rem(lax.axis_index("gy"), 2) == 0
    quarter = lane // 4
    columns = []
    for half in range(2):
        picked = []
        for g in range(4):
            acc = jnp.zeros((SUB, LANE), jnp.float32)
            for m in range(32):
                acc = jnp.where(
                    quarter == m, lanes(c_ref[4 * m + g, 8 * half : 8 * half + 8, :], 4 * m + 2), acc
                )
            picked.append(acc)
        found = []
        for j in range(4):
            out = lanes(picked[0], -j)
            for g in range(1, 4):
                out = jnp.where(lane % 4 == g, lanes(picked[g], g - j), out)
            found.append(out)
        columns.append(found)
    even = lane % 2 == 0
    first, last = [], []
    for ref in (cx_ref, cy_ref, vd_ref, em_ref):
        acc = jnp.zeros((SUB, LANE), jnp.float32)
        for k in range(64):
            acc = jnp.where(lane // 2 == k, lanes(ref[k], 2 * k + 1), acc)
        turned = subs(acc, 4)
        at_even = jnp.where(low, acc, turned)
        at_odd = jnp.where(low, turned, acc)
        last.append(jnp.where(even, at_even, lanes(at_odd, 1)))
        first.append(jnp.where(even, lanes(at_even, -1), at_odd))
    sides = []
    for (outer, inner), coefs in (((2, 3), first), ((1, 0), last)):
        pull = fluid * (coefs[0] + cross_diff)
        sides.append(
            [
                columns[0][outer],
                columns[1][outer],
                columns[0][inner],
                columns[1][inner],
                jnp.where(low, pull, coefs[1]),
                jnp.where(low, coefs[2], coefs[3]),
            ]
        )
    for n in range(6):
        to_left, to_right = sides[0][n], sides[1][n]
        a_ref[n] = jnp.where(even_gy, to_right, to_left)
        b_ref[n] = jnp.where(even_gy, to_left, to_right)


def factor_kernel(cx_ref, building_ref, inv_ref, prod_ref, ends_ref):
    fluid = fluid_of(building_ref)
    push = cross_diff * fluid

    def rows(k, state):
        ratio, from_prev, chain, first_prev = state
        for u in range(4):
            for r, wind in enumerate(both_rows(cx_ref[4 * k + u])):
                row = 8 * k + 2 * u + r
                pull = fluid * (wind + cross_diff)
                inv = 1.0 / ((1.0 + pull + push) - pull * ratio)
                from_prev = pull * inv * from_prev
                first_prev = first_prev + chain * from_prev
                ratio = push * inv
                chain = chain * ratio
                inv_ref[row] = inv
                prod_ref[row] = from_prev
        return ratio, from_prev, chain, first_prev

    zero = jnp.zeros((SUB, LANE), jnp.float32)
    ratio, from_prev, chain, first_prev = lax.fori_loop(0, 16, rows, (zero, zero + 1.0, zero + 1.0, zero))
    low = sub_ids() < 4
    ends_ref[0] = jnp.where(low, first_prev, chain)
    ends_ref[1] = jnp.where(low, from_prev, ratio)


def ghost_column(q, left, right, pull, wind, face, emitted):
    lane, sub = lane_ids(), sub_ids()
    fluid = jnp.where(pull > 0.0, 1.0, 0.0)
    face_up = level_above(face)
    sources = [
        jnp.where(sub == 0, emitted, jnp.where(sub == 4, subs(emitted, -1), 0.0)),
        jnp.where(sub == 0, subs(emitted, -2), jnp.where(sub == 4, subs(emitted, -3), 0.0)),
    ]
    inv = 1.0 / (1.0 + pull + cross_diff * fluid)
    lower = pull * inv
    upper = cross_diff * fluid * inv
    sides = [
        inv * side_of(q[h], left[h], right[h], wind, face, face_up, sources[h], fluid) for h in range(2)
    ]
    sides.append(jnp.where(lane == 0, lower, 0.0))
    sides.append(jnp.where(lane == LANE - 1, upper, 0.0))
    lower = jnp.where(lane == 0, 0.0, lower)
    upper = jnp.where(lane == LANE - 1, 0.0, upper)
    step = 1
    while step < LANE:
        low_prev, up_prev = lanes(lower, step), lanes(upper, step)
        low_next, up_next = lanes(lower, -step), lanes(upper, -step)
        inv = 1.0 / (1.0 - lower * up_prev - upper * low_next)
        lower, upper, from_low, from_up = inv * lower * low_prev, inv * upper * up_next, inv * lower, inv * upper
        sides = [inv * s + from_low * lanes(s, step) + from_up * lanes(s, -step) for s in sides]
        step *= 2
    return sides


def side_kernel(
    c_ref, cx_ref, cy_ref, vd_ref, em_ref, inv_ref, ends_ref, building_ref,
    sent_a_ref, sent_b_ref, got_a_ref, got_b_ref,
    side_ref, partial_ref, ghost_ref, rows_ref,
):
    lane, sub = lane_ids(), sub_ids()
    low = sub < 4
    fluid = fluid_of(building_ref)
    push = cross_diff * fluid
    even_gy = lax.rem(lax.axis_index("gy"), 2) == 0
    own_left = [jnp.where(even_gy, sent_b_ref[n], sent_a_ref[n]) for n in range(2)]
    own_right = [jnp.where(even_gy, sent_a_ref[n], sent_b_ref[n]) for n in range(2)]
    from_left = [jnp.where(even_gy, got_b_ref[n], got_a_ref[n]) for n in range(6)]
    from_right = [jnp.where(even_gy, got_a_ref[n], got_b_ref[n]) for n in range(6)]

    extra = jnp.zeros((SUB, LANE), jnp.float32)
    for s, (got, own) in enumerate(((from_left, own_left), (from_right, own_right))):
        left, right = (got[2:4], own) if s == 0 else (own, got[2:4])
        pull, wind = both_rows(got[4])
        face, emitted = both_rows(got[5])
        parts = ghost_column(got[0:2], left, right, pull, wind, face, emitted)
        for n in range(4):
            ghost_ref[4 * s + n] = parts[n]
        ends = [
            (parts[0], 0), (parts[1], 0), (parts[0], 1), (parts[1], 1),
            (parts[2], 0), (parts[3], 0), (parts[2], 1), (parts[3], 1),
        ]
        for j, (part, tail) in enumerate(ends):
            extra = jnp.where(lane == 2 * j + s, lanes(part, 2 * j + s + tail), extra)

    def rows(k, state):
        west, east, last, first, chain = state
        for u in range(4):
            pair = 4 * k + u
            pulls = both_rows(cx_ref[pair])
            winds = both_rows(cy_ref[pair])
            faces = both_rows(vd_ref[pair])
            for r in range(2):
                row = 2 * pair + r
                face_up = level_above(faces[r])
                inv = inv_ref[row]
                from_last = fluid * (pulls[r] + cross_diff) * inv
                new_last, new_first = [], []
                for h in range(2):
                    q = c_ref[row, 8 * h : 8 * h + 8, :]
                    left = jnp.where(lane == 0, lanes(west[h], -(2 * u + r)), lanes(q, 1))
                    right = jnp.where(lane == LANE - 1, lanes(east[h], -(2 * u + r) - 1), lanes(q, -1))
                    low_tracer = em_ref[pair, 4 * r + 2 * h : 4 * r + 2 * h + 1, :]
                    high_tracer = em_ref[pair, 4 * r + 2 * h + 1 : 4 * r + 2 * h + 2, :]
                    source = jnp.where(sub == 0, low_tracer, jnp.where(sub == 4, high_tracer, 0.0))
                    side = side_of(q, left, right, winds[r], faces[r], face_up, source, fluid)
                    value = side * inv + from_last * last[h]
                    side_ref[row, 8 * h : 8 * h + 8, :] = side
                    partial_ref[row, 8 * h : 8 * h + 8, :] = value
                    new_last.append(value)
                    new_first.append(first[h] + chain * value)
                last, first = new_last, new_first
                chain = chain * (push * inv)
        west = [lanes(x, -8) for x in west]
        east = [lanes(x, -8) for x in east]
        return west, east, last, first, chain

    zero = jnp.zeros((SUB, LANE), jnp.float32)
    start = (from_left[0:2], from_right[0:2], [zero, zero], [zero, zero], zero + 1.0)
    _, _, last, first, _ = lax.fori_loop(0, 16, rows, start)
    rows_ref[0], rows_ref[1] = first
    rows_ref[2], rows_ref[3] = last
    rows_ref[4] = ends_ref[0]
    rows_ref[5] = ends_ref[1]
    rows_ref[6] = extra


def interface(blocks, place):
    zero = jnp.zeros((SUB, LANE), jnp.float32)
    own, slope = [zero, zero], zero
    kept_own, kept_slope = own, slope
    forms = []
    for k, (first, last, first_prev, first_next, last_prev, last_next) in enumerate(blocks):
        here = place == k
        kept_own = [jnp.where(here, own[h], kept_own[h]) for h in range(2)]
        kept_slope = jnp.where(here, slope, kept_slope)
        inv = 1.0 / (1.0 - first_prev * slope)
        start = [(first[h] + first_prev * own[h]) * inv for h in range(2)]
        start_next = first_next * inv
        forms.append((start, start_next))
        carried = last_prev * slope
        own = [last[h] + last_prev * own[h] + carried * start[h] for h in range(2)]
        slope = last_next + carried * start_next
    after = [zero, zero]
    following, mine = after, after
    for k in reversed(range(len(forms))):
        following = [jnp.where(place == k, after[h], following[h]) for h in range(2)]
        start, start_next = forms[k]
        after = [start[h] + start_next * after[h] for h in range(2)]
        mine = [jnp.where(place == k, after[h], mine[h]) for h in range(2)]
    preceding = [kept_own[h] + kept_slope * mine[h] for h in range(2)]
    return preceding, following


def finish_kernel(
    blocks, side_ref, partial_ref, cy_ref, vd_ref, inv_ref, prod_ref, ghost_ref, rows_ref, building_ref, out_ref
):
    lane = lane_ids()
    fluid = fluid_of(building_ref)
    push = cross_diff * fluid
    place = lax.axis_index("gx")
    main, extra = [], []
    for k in range(blocks):
        first_prev, first_next = both_rows(rows_ref[k, 4])
        last_prev, last_next = both_rows(rows_ref[k, 5])
        main.append(
            ([rows_ref[k, 0], rows_ref[k, 1]], [rows_ref[k, 2], rows_ref[k, 3]],
             first_prev, first_next, last_prev, last_next)
        )
        e = [lanes(rows_ref[k, 6], -2 * j) for j in range(8)]
        extra.append((e[0:2], e[2:4], e[4], e[5], e[6], e[7]))
    preceding, following = interface(main, place)
    ghost_prev, ghost_next = interface(extra, place)
    ghosts = []
    for s in range(2):
        ghosts.append(
            [
                ghost_ref[4 * s + h]
                + ghost_ref[4 * s + 2] * ghost_prev[h][:, s : s + 1]
                + ghost_ref[4 * s + 3] * ghost_next[h][:, s : s + 1]
                for h in range(2)
            ]
        )
    west = [lanes(x, 8) for x in ghosts[0]]
    east = [lanes(x, 8) for x in ghosts[1]]

    def rows(step, state):
        k = 15 - step
        west, east, after = state
        for u in reversed(range(4)):
            pair = 4 * k + u
            winds = both_rows(cy_ref[pair])
            faces = both_rows(vd_ref[pair])
            for r in reversed(range(2)):
                row = 2 * pair + r
                face = faces[r]
                face_up = level_above(face)
                inv = 1.0 / (1.0 + face + face_up)
                lower = jnp.where(sub_ids() % 4 == 0, 0.0, face * inv)
                upper = face_up * inv
                inv_near = 1.0 / (1.0 - lower * subs(upper, 1) - upper * subs(lower, -1))
                near_low, near_up = inv_near * lower, inv_near * upper
                far_low, far_up = near_low * subs(lower, 1), near_up * subs(upper, -1)
                inv_far = 1.0 / (1.0 - far_low * subs(far_up, 2) - far_up * subs(far_low, -2))
                scale = inv_far * inv_near
                far_low, far_up = inv_far * far_low, inv_far * far_up
                ratio = push * inv_ref[row]
                from_prev = prod_ref[row]
                for h in range(2):
                    at = slice(8 * h, 8 * h + 8)
                    star = partial_ref[row, at, :] + from_prev * preceding[h] + ratio * after[h]
                    left = jnp.where(lane == 0, lanes(west[h], -(2 * u + r)), lanes(star, 1))
                    right = jnp.where(lane == LANE - 1, lanes(east[h], -(2 * u + r) - 1), lanes(star, -1))
                    side = 2.0 * star - side_ref[row, at, :] + span_operator(star, left, right, winds[r])
                    side = fluid * side * inv
                    near = inv_near * side + near_low * subs(side, 1) + near_up * subs(side, -1)
                    out_ref[row, at, :] = inv_far * near + far_low * subs(near, 2) + far_up * subs(near, -2)
                    after = [star if n == h else after[n] for n in range(2)]
        west = [lanes(x, 8) for x in west]
        east = [lanes(x, 8) for x in east]
        return west, east, after

    lax.fori_loop(0, 16, rows, (west, east, following))


def call(kernel, out_shapes, in_specs, flops, bytes_accessed):
    return pl.pallas_call(
        kernel,
        out_shape=[jax.ShapeDtypeStruct(shape, jnp.float32) for shape in out_shapes],
        in_specs=in_specs,
        out_specs=[VMEM] * len(out_shapes),
        compiler_params=pltpu.CompilerParams(vmem_limit_bytes=LIMIT),
        cost_estimate=pl.CostEstimate(flops=flops, bytes_accessed=bytes_accessed, transcendentals=0),
    )


def on_device(concentration, courant_x, courant_y, vert_diff, emission, building):
    cells, tracers, levels, span = concentration.shape
    blocks = lax.axis_size("gx")
    devices = lax.axis_size("gy")
    c = concentration.reshape(cells, tracers * levels, span)
    cx, cy, vd, em = (
        x.reshape(cells // 2, 2 * levels, span) for x in (courant_x, courant_y, vert_diff, emission)
    )
    row = (cells, SUB, LANE)
    field = (cells, 2 * SUB, LANE)
    packed = (6, SUB, LANE)
    sent_a, sent_b = call(pack_kernel, [packed, packed], [VMEM] * 5 + [SMEM], 10**6, 2 * 10**6)(
        c, cx, cy, vd, em, building
    )
    pairs_a = [(i, i + 1) for i in range(0, devices, 2)]
    pairs_b = [(i, (i + 1) % devices) for i in range(1, devices, 2)]
    got_a = lax.ppermute(sent_a, "gy", pairs_a + [(b, a) for a, b in pairs_a])
    got_b = lax.ppermute(sent_b, "gy", pairs_b + [(b, a) for a, b in pairs_b])
    inv, prod, ends = call(factor_kernel, [row, row, (2, SUB, LANE)], [VMEM, SMEM], 10**7, 10**7)(cx, building)
    side, partial, ghost, mine = call(
        side_kernel, [field, field, (8, SUB, LANE), (7, SUB, LANE)], [VMEM] * 7 + [SMEM] + [VMEM] * 4, 10**7, 10**7
    )(c, cx, cy, vd, em, inv, ends, building, sent_a, sent_b, got_a, got_b)
    gathered = lax.all_gather(mine, "gx")
    (updated,) = call(
        functools.partial(finish_kernel, blocks), [field], [VMEM] * 8 + [SMEM], 10**7, 10**7
    )(side, partial, cy, vd, inv, prod, ghost, gathered, building)
    return updated.reshape(concentration.shape)


def solution(mesh):
    in_specs = (
        P("gx", None, None, "gy"),
        P("gx", None, "gy"),
        P("gx", None, "gy"),
        P("gx", None, "gy"),
        P("gx", None, "gy"),
        P("gx", "gy"),
    )
    return jax.shard_map(
        on_device, mesh=mesh, in_specs=in_specs, out_specs=P("gx", None, None, "gy"), check_vma=False
    )
```

```python
import functools

import jax
import jax.numpy as jnp
from jax import lax
from jax.experimental import pallas as pl
from jax.experimental.pallas import tpu as pltpu
from jax.sharding import PartitionSpec as P

cross_diff = 300.0
span_diff = 0.25

SUB, LANE = 8, 128
VMEM = pl.BlockSpec(memory_space=pltpu.VMEM)
HBM = pl.BlockSpec(memory_space=pltpu.HBM)
SMEM = pl.BlockSpec(memory_space=pltpu.SMEM)
LIMIT = 16 * 1024 * 1024
(INV, PULLED, FROM_PREV, WEST, EAST, CENTRE, BELOW, ABOVE, NEAR, NEAR_LOW, NEAR_UP, FAR, FAR_LOW, FAR_UP) = range(14)
KEPT = 14
CHUNKS = 4


def sub_ids():
    return lax.broadcasted_iota(jnp.int32, (SUB, LANE), 0)


def lane_ids():
    return lax.broadcasted_iota(jnp.int32, (SUB, LANE), 1)


def lanes(x, shift):
    shift %= LANE
    return pltpu.roll(x, shift, 1) if shift else x


def subs(x, shift):
    shift %= SUB
    return pltpu.roll(x, shift, 0) if shift else x


def fluid_of(building_ref):
    return 1.0 - building_ref[0, 0].astype(jnp.float32)


def both_rows(pair):
    low = sub_ids() < 4
    turned = subs(pair, 4)
    return jnp.where(low, pair, turned), jnp.where(low, turned, pair)


def level_above(x):
    return jnp.where(sub_ids() % 4 == 3, 0.0, subs(x, -1))


def level_below(x):
    return jnp.where(sub_ids() % 4 == 0, 0.0, subs(x, 1))


def edge_quads(west, east):
    at_west = lane_ids() % 4 == 2
    return [jnp.where(at_west, lanes(west, 2 - g), lanes(east, 1 - g)) for g in range(4)]


def neighbours(q, quads, row):
    base, offset = row
    edge = pltpu.roll(quads[offset % 4], 126 - base - offset // 4 * 4, 1)
    lane = lane_ids()
    return jnp.where(lane == 0, edge, lanes(q, 1)), jnp.where(lane == LANE - 1, edge, lanes(q, -1))


def pack_kernel(
    c_hbm, cx_hbm, cy_hbm, vd_hbm, em_hbm, building_ref,
    a_ref, b_ref, c_ref, cx_ref, cy_ref, vd_ref, em_ref, sems,
):
    coefs = ((cx_hbm, cx_ref), (cy_hbm, cy_ref), (vd_hbm, vd_ref), (em_hbm, em_ref))
    size = c_ref.shape[0] // CHUNKS
    copies = [
        pltpu.make_async_copy(c_hbm.at[pl.ds(n * size, size)], c_ref.at[pl.ds(n * size, size)], sems.at[n])
        for n in range(CHUNKS)
    ]
    copies += [pltpu.make_async_copy(src, dst, sems.at[CHUNKS + n]) for n, (src, dst) in enumerate(coefs)]
    for copy in copies:
        copy.start()

    lane, sub = lane_ids(), sub_ids()
    fluid = fluid_of(building_ref)
    low = sub < 4
    even_gy = lax.rem(lax.axis_index("gy"), 2) == 0
    quarter = lane // 4
    zero = jnp.zeros((SUB, LANE), jnp.float32)
    picked = [[zero] * 4 for _ in range(2)]
    for n in range(CHUNKS):
        copies[n].wait()
        for m in range(n * size // 4, (n + 1) * size // 4):
            here = quarter == m
            for g in range(4):
                for half in range(2):
                    turned = lanes(c_ref[4 * m + g, 8 * half : 8 * half + 8, :], 4 * m + 2)
                    picked[half][g] = jnp.where(here, turned, picked[half][g])
    columns = []
    for half in range(2):
        found = []
        for j in range(4):
            out = lanes(picked[half][0], -j)
            for g in range(1, 4):
                out = jnp.where(lane % 4 == g, lanes(picked[half][g], g - j), out)
            found.append(out)
        columns.append(found)
    even = lane % 2 == 0
    pair_of = lane // 2
    first, last = [], []
    for n, (_, ref) in enumerate(coefs):
        copies[CHUNKS + n].wait()
        acc = zero
        for k in range(64):
            acc = jnp.where(pair_of == k, lanes(ref[k], 2 * k + 1), acc)
        turned = subs(acc, 4)
        at_even = jnp.where(low, acc, turned)
        at_odd = jnp.where(low, turned, acc)
        last.append(jnp.where(even, at_even, lanes(at_odd, 1)))
        first.append(jnp.where(even, lanes(at_even, -1), at_odd))
    sides = []
    for (outer, inner), edge in (((2, 3), first), ((1, 0), last)):
        pull = fluid * (edge[0] + cross_diff)
        sides.append(
            [
                columns[0][outer],
                columns[1][outer],
                columns[0][inner],
                columns[1][inner],
                jnp.where(low, pull, edge[1]),
                jnp.where(low, edge[2], edge[3]),
            ]
        )
    for n in range(6):
        to_left, to_right = sides[0][n], sides[1][n]
        a_ref[n] = jnp.where(even_gy, to_right, to_left)
        b_ref[n] = jnp.where(even_gy, to_left, to_right)


def factor_kernel(cx_ref, cy_ref, vd_ref, building_ref, kept_ref, ends_ref):
    fluid = fluid_of(building_ref)
    push = cross_diff * fluid
    ground = sub_ids() % 4 == 0

    def rows(k, state):
        ratio, from_prev, chain, first_prev = state
        for u in range(4):
            pair = 4 * k + u
            wind, face = cy_ref[pair], vd_ref[pair]
            face_up = level_above(face)
            west = fluid * (jnp.maximum(wind, 0.0) + span_diff)
            east = fluid * (jnp.maximum(-wind, 0.0) + span_diff)
            inv = 1.0 / (1.0 + face + face_up)
            lower = jnp.where(ground, 0.0, face * inv)
            upper = face_up * inv
            near = 1.0 / (1.0 - lower * subs(upper, 1) - upper * subs(lower, -1))
            near_low, near_up = near * lower, near * upper
            far_low, far_up = near_low * subs(lower, 1), near_up * subs(upper, -1)
            far = 1.0 / (1.0 - far_low * subs(far_up, 2) - far_up * subs(far_low, -2))
            scale = fluid * inv
            pairs = {
                WEST: west,
                EAST: east,
                CENTRE: fluid * (1.0 - face - face_up) - west - east,
                BELOW: jnp.where(ground, 0.0, fluid * face),
                ABOVE: fluid * face_up,
                NEAR: near * scale,
                NEAR_LOW: near_low * subs(scale, 1),
                NEAR_UP: near_up * subs(scale, -1),
                FAR: far,
                FAR_LOW: far * far_low,
                FAR_UP: far * far_up,
            }
            for n, value in pairs.items():
                kept_ref[2 * pair, n], kept_ref[2 * pair + 1, n] = both_rows(value)
            for r, pull in enumerate(both_rows(fluid * (cx_ref[pair] + cross_diff))):
                row = 2 * pair + r
                inv = 1.0 / ((1.0 + pull + push) - pull * ratio)
                pulled = pull * inv
                from_prev = pulled * from_prev
                first_prev = first_prev + chain * from_prev
                ratio = push * inv
                chain = chain * ratio
                kept_ref[row, INV] = inv
                kept_ref[row, PULLED] = pulled
                kept_ref[row, FROM_PREV] = from_prev
        return ratio, from_prev, chain, first_prev

    zero = jnp.zeros((SUB, LANE), jnp.float32)
    ratio, from_prev, chain, first_prev = lax.fori_loop(0, 16, rows, (zero, zero + 1.0, zero + 1.0, zero))
    low = sub_ids() < 4
    ends_ref[0] = jnp.where(low, first_prev, chain)
    ends_ref[1] = jnp.where(low, from_prev, ratio)


def merge(left, right, part):
    low = sub_ids() < 4
    return jnp.where(low, left, subs(right, 4)) if part == 0 else jnp.where(low, subs(left, 4), right)


def ghost_columns(from_left, from_right, own_left, own_right):
    lane, sub = lane_ids(), sub_ids()
    pull, wind = merge(from_left[4], from_right[4], 0), merge(from_left[4], from_right[4], 1)
    face, emitted = merge(from_left[5], from_right[5], 0), merge(from_left[5], from_right[5], 1)
    fluid = jnp.where(pull > 0.0, 1.0, 0.0)
    face_up = level_above(face)
    west = jnp.maximum(wind, 0.0) + span_diff
    east = jnp.maximum(-wind, 0.0) + span_diff
    inv = 1.0 / (1.0 + pull + cross_diff * fluid)
    lower = pull * inv
    upper = cross_diff * fluid * inv
    sides = []
    for t in range(4):
        h, part = t // 2, t % 2
        q = merge(from_left[h], from_right[h], part)
        left = merge(from_left[2 + h], own_right[h], part)
        right = merge(own_left[h], from_right[2 + h], part)
        side = q + west * (left - q) + east * (right - q)
        side = side + face * (level_below(q) - q) + face_up * (level_above(q) - q)
        side = side + jnp.where(sub % 4 == 0, subs(emitted, -t), 0.0)
        sides.append(inv * fluid * side)
    sides.append(jnp.where(lane == 0, lower, 0.0))
    sides.append(jnp.where(lane == LANE - 1, upper, 0.0))
    lower = jnp.where(lane == 0, 0.0, lower)
    upper = jnp.where(lane == LANE - 1, 0.0, upper)
    step = 1
    while step < LANE:
        low_prev, up_prev = lanes(lower, step), lanes(upper, step)
        low_next, up_next = lanes(lower, -step), lanes(upper, -step)
        inv = 1.0 / (1.0 - lower * up_prev - upper * low_next)
        from_low, from_up = inv * lower, inv * upper
        sides = [inv * s + from_low * lanes(s, step) + from_up * lanes(s, -step) for s in sides]
        lower, upper = from_low * low_prev, from_up * up_next
        step *= 2
    prev, following = both_rows(sides[4]), both_rows(sides[5])
    return [
        [merge(sides[0], sides[1], s), merge(sides[2], sides[3], s), prev[s], following[s]] for s in range(2)
    ]


def side_kernel(
    c_ref, em_ref, kept_ref, ends_ref, building_ref, sent_a_ref, sent_b_ref, got_a_ref, got_b_ref,
    side_ref, partial_ref, ghost_ref, rows_ref,
):
    lane, sub = lane_ids(), sub_ids()
    fluid = fluid_of(building_ref)
    push = cross_diff * fluid
    even_gy = lax.rem(lax.axis_index("gy"), 2) == 0
    own_left = [jnp.where(even_gy, sent_b_ref[n], sent_a_ref[n]) for n in range(2)]
    own_right = [jnp.where(even_gy, sent_a_ref[n], sent_b_ref[n]) for n in range(2)]
    from_left = [jnp.where(even_gy, got_b_ref[n], got_a_ref[n]) for n in range(6)]
    from_right = [jnp.where(even_gy, got_a_ref[n], got_b_ref[n]) for n in range(6)]

    extra = jnp.zeros((SUB, LANE), jnp.float32)
    for s, parts in enumerate(ghost_columns(from_left, from_right, own_left, own_right)):
        for n in range(4):
            ghost_ref[4 * s + n] = parts[n]
        ends = [
            (parts[0], 0), (parts[1], 0), (parts[0], 1), (parts[1], 1),
            (parts[2], 0), (parts[3], 0), (parts[2], 1), (parts[3], 1),
        ]
        for j, (part, tail) in enumerate(ends):
            extra = jnp.where(lane == 2 * j + s, lanes(part, 2 * j + s + tail), extra)

    quads = [edge_quads(from_left[h], from_right[h]) for h in range(2)]

    def rows(k, state):
        last, first, chain = state
        for n in range(8):
            row, pair = 8 * k + n, 4 * k + n // 2
            inv, pulled = kept_ref[row, INV], kept_ref[row, PULLED]
            west, east, centre = kept_ref[row, WEST], kept_ref[row, EAST], kept_ref[row, CENTRE]
            below, above = kept_ref[row, BELOW], kept_ref[row, ABOVE]
            new_last, new_first = [], []
            for h in range(2):
                q = c_ref[row, 8 * h : 8 * h + 8, :]
                left, right = neighbours(q, quads[h], (8 * k, n))
                tracer = 4 * (n % 2) + 2 * h
                source = jnp.where(
                    sub == 0,
                    em_ref[pair, tracer : tracer + 1, :],
                    jnp.where(sub == 4, em_ref[pair, tracer + 1 : tracer + 2, :], 0.0),
                )
                side = (centre * q + fluid * source) + (west * left + east * right)
                side = side + (below * subs(q, 1) + above * subs(q, -1))
                value = side * inv + pulled * last[h]
                side_ref[row, 8 * h : 8 * h + 8, :] = side
                partial_ref[row, 8 * h : 8 * h + 8, :] = value
                new_last.append(value)
                new_first.append(first[h] + chain * value)
            last, first = new_last, new_first
            chain = chain * (push * inv)
        return last, first, chain

    zero = jnp.zeros((SUB, LANE), jnp.float32)
    last, first, _ = lax.fori_loop(0, 16, rows, ([zero, zero], [zero, zero], zero + 1.0))
    rows_ref[0], rows_ref[1] = first
    rows_ref[2], rows_ref[3] = last
    rows_ref[4] = ends_ref[0]
    rows_ref[5] = ends_ref[1]
    rows_ref[6] = extra


def interface(blocks, place):
    zero = jnp.zeros((SUB, LANE), jnp.float32)
    own, slope = [zero, zero], zero
    kept_own, kept_slope = own, slope
    forms = []
    for k, (first, last, first_prev, first_next, last_prev, last_next) in enumerate(blocks):
        here = place == k
        kept_own = [jnp.where(here, own[h], kept_own[h]) for h in range(2)]
        kept_slope = jnp.where(here, slope, kept_slope)
        inv = 1.0 / (1.0 - first_prev * slope)
        start = [(first[h] + first_prev * own[h]) * inv for h in range(2)]
        start_next = first_next * inv
        forms.append((start, start_next))
        carried = last_prev * slope
        own = [last[h] + last_prev * own[h] + carried * start[h] for h in range(2)]
        slope = last_next + carried * start_next
    after = [zero, zero]
    following, mine = after, after
    for k in reversed(range(len(forms))):
        following = [jnp.where(place == k, after[h], following[h]) for h in range(2)]
        start, start_next = forms[k]
        after = [start[h] + start_next * after[h] for h in range(2)]
        mine = [jnp.where(place == k, after[h], mine[h]) for h in range(2)]
    preceding = [kept_own[h] + kept_slope * mine[h] for h in range(2)]
    return preceding, following


def finish_kernel(blocks, side_ref, partial_ref, kept_ref, ghost_ref, rows_ref, building_ref, out_ref):
    push = cross_diff * fluid_of(building_ref)
    place = lax.axis_index("gx")
    main, extra = [], []
    for k in range(blocks):
        first_prev, first_next = both_rows(rows_ref[k, 4])
        last_prev, last_next = both_rows(rows_ref[k, 5])
        main.append(
            ([rows_ref[k, 0], rows_ref[k, 1]], [rows_ref[k, 2], rows_ref[k, 3]],
             first_prev, first_next, last_prev, last_next)
        )
        e = [lanes(rows_ref[k, 6], -2 * j) for j in range(8)]
        extra.append((e[0:2], e[2:4], e[4], e[5], e[6], e[7]))
    preceding, following = interface(main, place)
    ghost_prev, ghost_next = interface(extra, place)
    ghosts = []
    for s in range(2):
        ghosts.append(
            [
                ghost_ref[4 * s + h]
                + ghost_ref[4 * s + 2] * ghost_prev[h][:, s : s + 1]
                + ghost_ref[4 * s + 3] * ghost_next[h][:, s : s + 1]
                for h in range(2)
            ]
        )
    quads = [edge_quads(ghosts[0][h], ghosts[1][h]) for h in range(2)]

    def rows(step, after):
        k = 15 - step
        for n in reversed(range(8)):
            row = 8 * k + n
            ratio, from_prev = push * kept_ref[row, INV], kept_ref[row, FROM_PREV]
            west, east = kept_ref[row, WEST], kept_ref[row, EAST]
            near, near_low, near_up = kept_ref[row, NEAR], kept_ref[row, NEAR_LOW], kept_ref[row, NEAR_UP]
            far, far_low, far_up = kept_ref[row, FAR], kept_ref[row, FAR_LOW], kept_ref[row, FAR_UP]
            centre = 2.0 - west - east
            new_after = []
            for h in range(2):
                at = slice(8 * h, 8 * h + 8)
                star = (partial_ref[row, at, :] + from_prev * preceding[h]) + ratio * after[h]
                left, right = neighbours(star, quads[h], (8 * k, n))
                side = (centre * star - side_ref[row, at, :]) + (west * left + east * right)
                value = near * side + near_low * subs(side, 1) + near_up * subs(side, -1)
                out_ref[row, at, :] = far * value + far_low * subs(value, 2) + far_up * subs(value, -2)
                new_after.append(star)
            after = new_after
        return after

    lax.fori_loop(0, 16, rows, following)


def call(kernel, out_shapes, in_specs, flops, bytes_accessed, limit=LIMIT, scratch=()):
    return pl.pallas_call(
        kernel,
        out_shape=[jax.ShapeDtypeStruct(shape, jnp.float32) for shape in out_shapes],
        in_specs=in_specs,
        out_specs=[VMEM] * len(out_shapes),
        scratch_shapes=list(scratch),
        compiler_params=pltpu.CompilerParams(vmem_limit_bytes=limit),
        cost_estimate=pl.CostEstimate(flops=flops, bytes_accessed=bytes_accessed, transcendentals=0),
    )


def on_device(concentration, courant_x, courant_y, vert_diff, emission, building):
    cells, tracers, levels, span = concentration.shape
    blocks = lax.axis_size("gx")
    devices = lax.axis_size("gy")
    c = concentration.reshape(cells, tracers * levels, span)
    coefs = [x.reshape(cells // 2, 2 * levels, span) for x in (courant_x, courant_y, vert_diff, emission)]
    field = (cells, 2 * SUB, LANE)
    packed = (6, SUB, LANE)
    sent_a, sent_b, c, cx, cy, vd, em = call(
        pack_kernel,
        [packed, packed, field] + [x.shape for x in coefs],
        [HBM] * 5 + [SMEM],
        10**6,
        2 * 10**6,
        scratch=[pltpu.SemaphoreType.DMA((CHUNKS + 4,))],
    )(*(pltpu.with_memory_space_constraint(x, pltpu.HBM) for x in (c, *coefs)), building)
    pairs_a = [(i, i + 1) for i in range(0, devices, 2)]
    pairs_b = [(i, (i + 1) % devices) for i in range(1, devices, 2)]
    got_a = lax.ppermute(sent_a, "gy", pairs_a + [(b, a) for a, b in pairs_a])
    got_b = lax.ppermute(sent_b, "gy", pairs_b + [(b, a) for a, b in pairs_b])
    kept, ends = call(
        factor_kernel, [(cells, KEPT, SUB, LANE), (2, SUB, LANE)], [VMEM] * 3 + [SMEM], 10**7, 10**7
    )(cx, cy, vd, building)
    side, partial, ghost, mine = call(
        side_kernel, [field, field, (8, SUB, LANE), (7, SUB, LANE)], [VMEM] * 4 + [SMEM] + [VMEM] * 4, 10**7, 10**7
    )(c, em, kept, ends, building, sent_a, sent_b, got_a, got_b)
    gathered = lax.all_gather(mine, "gx")
    (updated,) = call(functools.partial(finish_kernel, blocks), [field], [VMEM] * 5 + [SMEM], 10**7, 10**7)(
        side, partial, kept, ghost, gathered, building
    )
    return updated.reshape(concentration.shape)


def solution(mesh):
    in_specs = (
        P("gx", None, None, "gy"),
        P("gx", None, "gy"),
        P("gx", None, "gy"),
        P("gx", None, "gy"),
        P("gx", None, "gy"),
        P("gx", "gy"),
    )
    return jax.shard_map(
        on_device, mesh=mesh, in_specs=in_specs, out_specs=P("gx", None, None, "gy"), check_vma=False
    )
```

```python
import functools

import jax
import jax.numpy as jnp
from jax import lax
from jax.experimental import pallas as pl
from jax.experimental.pallas import tpu as pltpu
from jax.sharding import PartitionSpec as P

cross_diff = 300.0
span_diff = 0.25

SUB, LANE = 8, 128
VMEM = pl.BlockSpec(memory_space=pltpu.VMEM)
HBM = pl.BlockSpec(memory_space=pltpu.HBM)
SMEM = pl.BlockSpec(memory_space=pltpu.SMEM)
LIMIT = 16 * 1024 * 1024
(INV, PULLED, FROM_PREV, WEST, EAST, CENTRE, BELOW, ABOVE, NEAR, NEAR_LOW, NEAR_UP, FAR, FAR_LOW, FAR_UP) = range(14)
KEPT = 14
CHUNKS = 4


def sub_ids():
    return lax.broadcasted_iota(jnp.int32, (SUB, LANE), 0)


def lane_ids():
    return lax.broadcasted_iota(jnp.int32, (SUB, LANE), 1)


def lanes(x, shift):
    shift %= LANE
    return pltpu.roll(x, shift, 1) if shift else x


def subs(x, shift):
    shift %= SUB
    return pltpu.roll(x, shift, 0) if shift else x


def fluid_of(building_ref):
    return 1.0 - building_ref[0, 0].astype(jnp.float32)


def both_rows(pair):
    low = sub_ids() < 4
    turned = subs(pair, 4)
    return jnp.where(low, pair, turned), jnp.where(low, turned, pair)


def level_above(x):
    return jnp.where(sub_ids() % 4 == 3, 0.0, subs(x, -1))


def level_below(x):
    return jnp.where(sub_ids() % 4 == 0, 0.0, subs(x, 1))


def edge_quads(west, east):
    at_west = lane_ids() % 4 == 2
    return [jnp.where(at_west, lanes(west, 2 - g), lanes(east, 1 - g)) for g in range(4)]


def neighbours(q, quads, row):
    base, offset = row
    edge = pltpu.roll(quads[offset % 4], 126 - base - offset // 4 * 4, 1)
    lane = lane_ids()
    return jnp.where(lane == 0, edge, lanes(q, 1)), jnp.where(lane == LANE - 1, edge, lanes(q, -1))


def pack_kernel(
    c_hbm, cx_hbm, cy_hbm, vd_hbm, em_hbm, building_ref,
    a_ref, b_ref, c_ref, cx_ref, cy_ref, vd_ref, em_ref, sems,
):
    coefs = ((cx_hbm, cx_ref), (cy_hbm, cy_ref), (vd_hbm, vd_ref), (em_hbm, em_ref))
    size = c_ref.shape[0] // CHUNKS
    copies = [
        pltpu.make_async_copy(c_hbm.at[pl.ds(n * size, size)], c_ref.at[pl.ds(n * size, size)], sems.at[n])
        for n in range(CHUNKS)
    ]
    copies += [pltpu.make_async_copy(src, dst, sems.at[CHUNKS + n]) for n, (src, dst) in enumerate(coefs)]
    for copy in copies:
        copy.start()

    lane, sub = lane_ids(), sub_ids()
    fluid = fluid_of(building_ref)
    low = sub < 4
    even_gy = lax.rem(lax.axis_index("gy"), 2) == 0
    quarter = lane // 4
    zero = jnp.zeros((SUB, LANE), jnp.float32)
    picked = [[zero] * 4 for _ in range(2)]
    for n in range(CHUNKS):
        copies[n].wait()
        for m in range(n * size // 4, (n + 1) * size // 4):
            here = quarter == m
            for g in range(4):
                for half in range(2):
                    turned = lanes(c_ref[4 * m + g, 8 * half : 8 * half + 8, :], 4 * m + 2)
                    picked[half][g] = jnp.where(here, turned, picked[half][g])
    columns = []
    for half in range(2):
        found = []
        for j in range(4):
            out = lanes(picked[half][0], -j)
            for g in range(1, 4):
                out = jnp.where(lane % 4 == g, lanes(picked[half][g], g - j), out)
            found.append(out)
        columns.append(found)
    even = lane % 2 == 0
    pair_of = lane // 2
    first, last = [], []
    for n, (_, ref) in enumerate(coefs):
        copies[CHUNKS + n].wait()
        acc = zero
        for k in range(64):
            acc = jnp.where(pair_of == k, lanes(ref[k], 2 * k + 1), acc)
        turned = subs(acc, 4)
        at_even = jnp.where(low, acc, turned)
        at_odd = jnp.where(low, turned, acc)
        last.append(jnp.where(even, at_even, lanes(at_odd, 1)))
        first.append(jnp.where(even, lanes(at_even, -1), at_odd))
    sides = []
    for (outer, inner), edge in (((2, 3), first), ((1, 0), last)):
        pull = fluid * (edge[0] + cross_diff)
        sides.append(
            [
                columns[0][outer],
                columns[1][outer],
                columns[0][inner],
                columns[1][inner],
                jnp.where(low, pull, edge[1]),
                jnp.where(low, edge[2], edge[3]),
            ]
        )
    for n in range(6):
        to_left, to_right = sides[0][n], sides[1][n]
        a_ref[n] = jnp.where(even_gy, to_right, to_left)
        b_ref[n] = jnp.where(even_gy, to_left, to_right)


def factor_kernel(cx_ref, cy_ref, vd_ref, building_ref, kept_ref, ends_ref):
    fluid = fluid_of(building_ref)
    push = cross_diff * fluid
    ground = sub_ids() % 4 == 0

    def rows(k, state):
        ratio, from_prev, chain, first_prev = state
        for u in range(4):
            pair = 4 * k + u
            wind, face = cy_ref[pair], vd_ref[pair]
            face_up = level_above(face)
            west = fluid * (jnp.maximum(wind, 0.0) + span_diff)
            east = fluid * (jnp.maximum(-wind, 0.0) + span_diff)
            inv = 1.0 / (1.0 + face + face_up)
            lower = jnp.where(ground, 0.0, face * inv)
            upper = face_up * inv
            near = 1.0 / (1.0 - lower * subs(upper, 1) - upper * subs(lower, -1))
            near_low, near_up = near * lower, near * upper
            far_low, far_up = near_low * subs(lower, 1), near_up * subs(upper, -1)
            far = 1.0 / (1.0 - far_low * subs(far_up, 2) - far_up * subs(far_low, -2))
            scale = fluid * inv
            pairs = {
                WEST: west,
                EAST: east,
                CENTRE: fluid * (1.0 - face - face_up) - west - east,
                BELOW: jnp.where(ground, 0.0, fluid * face),
                ABOVE: fluid * face_up,
                NEAR: near * scale,
                NEAR_LOW: near_low * subs(scale, 1),
                NEAR_UP: near_up * subs(scale, -1),
                FAR: far,
                FAR_LOW: far * far_low,
                FAR_UP: far * far_up,
            }
            for n, value in pairs.items():
                kept_ref[2 * pair, n], kept_ref[2 * pair + 1, n] = both_rows(value)
            for r, pull in enumerate(both_rows(fluid * (cx_ref[pair] + cross_diff))):
                row = 2 * pair + r
                inv = 1.0 / ((1.0 + pull + push) - pull * ratio)
                pulled = pull * inv
                from_prev = pulled * from_prev
                first_prev = first_prev + chain * from_prev
                ratio = push * inv
                chain = chain * ratio
                kept_ref[row, INV] = inv
                kept_ref[row, PULLED] = pulled
                kept_ref[row, FROM_PREV] = from_prev
        return ratio, from_prev, chain, first_prev

    zero = jnp.zeros((SUB, LANE), jnp.float32)
    ratio, from_prev, chain, first_prev = lax.fori_loop(0, 16, rows, (zero, zero + 1.0, zero + 1.0, zero))
    low = sub_ids() < 4
    ends_ref[0] = jnp.where(low, first_prev, chain)
    ends_ref[1] = jnp.where(low, from_prev, ratio)


def merge(left, right, part):
    low = sub_ids() < 4
    return jnp.where(low, left, subs(right, 4)) if part == 0 else jnp.where(low, subs(left, 4), right)


def ghost_columns(from_left, from_right, own_left, own_right):
    lane, sub = lane_ids(), sub_ids()
    pull, wind = merge(from_left[4], from_right[4], 0), merge(from_left[4], from_right[4], 1)
    face, emitted = merge(from_left[5], from_right[5], 0), merge(from_left[5], from_right[5], 1)
    fluid = jnp.where(pull > 0.0, 1.0, 0.0)
    face_up = level_above(face)
    west = jnp.maximum(wind, 0.0) + span_diff
    east = jnp.maximum(-wind, 0.0) + span_diff
    inv = 1.0 / (1.0 + pull + cross_diff * fluid)
    lower = pull * inv
    upper = cross_diff * fluid * inv
    sides = []
    for t in range(4):
        h, part = t // 2, t % 2
        q = merge(from_left[h], from_right[h], part)
        left = merge(from_left[2 + h], own_right[h], part)
        right = merge(own_left[h], from_right[2 + h], part)
        side = q + west * (left - q) + east * (right - q)
        side = side + face * (level_below(q) - q) + face_up * (level_above(q) - q)
        side = side + jnp.where(sub % 4 == 0, subs(emitted, -t), 0.0)
        sides.append(inv * fluid * side)
    sides.append(jnp.where(lane == 0, lower, 0.0))
    sides.append(jnp.where(lane == LANE - 1, upper, 0.0))
    lower = jnp.where(lane == 0, 0.0, lower)
    upper = jnp.where(lane == LANE - 1, 0.0, upper)
    step = 1
    while step < LANE:
        low_prev, up_prev = lanes(lower, step), lanes(upper, step)
        low_next, up_next = lanes(lower, -step), lanes(upper, -step)
        inv = 1.0 / (1.0 - lower * up_prev - upper * low_next)
        from_low, from_up = inv * lower, inv * upper
        sides = [inv * s + from_low * lanes(s, step) + from_up * lanes(s, -step) for s in sides]
        lower, upper = from_low * low_prev, from_up * up_next
        step *= 2
    prev, following = both_rows(sides[4]), both_rows(sides[5])
    return [
        [merge(sides[0], sides[1], s), merge(sides[2], sides[3], s), prev[s], following[s]] for s in range(2)
    ]


def side_kernel(
    c_ref, em_ref, kept_ref, ends_ref, building_ref, sent_b_ref, sent_a_ref, got_b_ref, got_a_ref,
    side_ref, partial_ref, ghost_ref, rows_ref,
):
    lane, sub = lane_ids(), sub_ids()
    fluid = fluid_of(building_ref)
    push = cross_diff * fluid
    even_gy = lax.rem(lax.axis_index("gy"), 2) == 0
    own_left = [jnp.where(even_gy, sent_b_ref[n], sent_a_ref[n]) for n in range(2)]
    own_right = [jnp.where(even_gy, sent_a_ref[n], sent_b_ref[n]) for n in range(2)]
    from_left = [jnp.where(even_gy, got_b_ref[n], got_a_ref[n]) for n in range(6)]
    from_right = [jnp.where(even_gy, got_a_ref[n], got_b_ref[n]) for n in range(6)]

    extra = jnp.zeros((SUB, LANE), jnp.float32)
    for s, parts in enumerate(ghost_columns(from_left, from_right, own_left, own_right)):
        for n in range(4):
            ghost_ref[4 * s + n] = parts[n]
        ends = [
            (parts[0], 0), (parts[1], 0), (parts[0], 1), (parts[1], 1),
            (parts[2], 0), (parts[3], 0), (parts[2], 1), (parts[3], 1),
        ]
        for j, (part, tail) in enumerate(ends):
            extra = jnp.where(lane == 2 * j + s, lanes(part, 2 * j + s + tail), extra)

    quads = [edge_quads(from_left[h], from_right[h]) for h in range(2)]

    def rows(k, state):
        last, first, chain = state
        for n in range(8):
            row, pair = 8 * k + n, 4 * k + n // 2
            inv, pulled = kept_ref[row, INV], kept_ref[row, PULLED]
            west, east, centre = kept_ref[row, WEST], kept_ref[row, EAST], kept_ref[row, CENTRE]
            below, above = kept_ref[row, BELOW], kept_ref[row, ABOVE]
            new_last, new_first = [], []
            for h in range(2):
                q = c_ref[row, 8 * h : 8 * h + 8, :]
                left, right = neighbours(q, quads[h], (8 * k, n))
                tracer = 4 * (n % 2) + 2 * h
                source = jnp.where(
                    sub == 0,
                    em_ref[pair, tracer : tracer + 1, :],
                    jnp.where(sub == 4, em_ref[pair, tracer + 1 : tracer + 2, :], 0.0),
                )
                side = (centre * q + fluid * source) + (west * left + east * right)
                side = side + (below * subs(q, 1) + above * subs(q, -1))
                value = side * inv + pulled * last[h]
                side_ref[row, 8 * h : 8 * h + 8, :] = side
                partial_ref[row, 8 * h : 8 * h + 8, :] = value
                new_last.append(value)
                new_first.append(first[h] + chain * value)
            last, first = new_last, new_first
            chain = chain * (push * inv)
        return last, first, chain

    zero = jnp.zeros((SUB, LANE), jnp.float32)
    last, first, _ = lax.fori_loop(0, 16, rows, ([zero, zero], [zero, zero], zero + 1.0))
    rows_ref[0], rows_ref[1] = first
    rows_ref[2], rows_ref[3] = last
    rows_ref[4] = ends_ref[0]
    rows_ref[5] = ends_ref[1]
    rows_ref[6] = extra


def blocks_of(rows_ref):
    main, extra = [], []
    for k in range(rows_ref.shape[0]):
        first_prev, first_next = both_rows(rows_ref[k, 4])
        last_prev, last_next = both_rows(rows_ref[k, 5])
        main.append(
            ([rows_ref[k, 0], rows_ref[k, 1]], [rows_ref[k, 2], rows_ref[k, 3]],
             first_prev, first_next, last_prev, last_next)
        )
        e = [lanes(rows_ref[k, 6], -2 * j) for j in range(8)]
        extra.append((e[0:2], e[2:4], e[4], e[5], e[6], e[7]))
    return main, extra


def joined(before, after):
    first, last, first_prev, first_next, last_prev, last_next = before
    first_b, last_b, first_prev_b, first_next_b, last_prev_b, last_next_b = after
    inv = 1.0 / (1.0 - last_next * first_prev_b)
    low_own = [(last[h] + last_next * first_b[h]) * inv for h in range(2)]
    low_prev, low_next = last_prev * inv, last_next * first_next_b * inv
    high_own = [first_b[h] + first_prev_b * low_own[h] for h in range(2)]
    high_prev, high_next = first_prev_b * low_prev, first_next_b + first_prev_b * low_next
    return (
        [first[h] + first_next * high_own[h] for h in range(2)],
        [last_b[h] + last_prev_b * low_own[h] for h in range(2)],
        first_prev + first_next * high_prev,
        first_next * high_next,
        last_prev_b * low_prev,
        last_next_b + last_prev_b * low_next,
    )


def condense_kernel(rows_ref, out_ref):
    main, extra = (functools.reduce(joined, forms) for forms in blocks_of(rows_ref))
    low, lane = sub_ids() < 4, lane_ids()
    out_ref[0], out_ref[1] = main[0]
    out_ref[2], out_ref[3] = main[1]
    out_ref[4] = jnp.where(low, main[2], main[3])
    out_ref[5] = jnp.where(low, main[4], main[5])
    packed = extra[0][0]
    for j, part in enumerate((extra[0][1], *extra[1], *extra[2:]), 1):
        packed = jnp.where(lane // 2 == j, lanes(part, 2 * j), packed)
    out_ref[6] = packed


def interface(blocks, place, before, beyond):
    zero = jnp.zeros((SUB, LANE), jnp.float32)
    own, slope = before, zero
    kept_own, kept_slope = own, slope
    forms = []
    for k, (first, last, first_prev, first_next, last_prev, last_next) in enumerate(blocks):
        if k:
            here = place == k
            kept_own = [jnp.where(here, own[h], kept_own[h]) for h in range(2)]
            kept_slope = jnp.where(here, slope, kept_slope)
        inv = 1.0 / (1.0 - first_prev * slope)
        start = [(first[h] + first_prev * own[h]) * inv for h in range(2)]
        start_next = first_next * inv
        forms.append((start, start_next))
        carried = last_prev * slope
        own = [last[h] + last_prev * own[h] + carried * start[h] for h in range(2)]
        slope = last_next + carried * start_next
    after = beyond
    following, mine = after, after
    for k in reversed(range(len(forms))):
        following = [jnp.where(place == k, after[h], following[h]) for h in range(2)]
        start, start_next = forms[k]
        after = [start[h] + start_next * after[h] for h in range(2)]
        mine = [jnp.where(place == k, after[h], mine[h]) for h in range(2)]
    preceding = [kept_own[h] + kept_slope * mine[h] for h in range(2)]
    return preceding, following


def finish_kernel(
    side_ref, partial_ref, kept_ref, ghost_ref, near_ref, pair_ref, half_ref, building_ref, out_hbm, out_ref, sems
):
    push = cross_diff * fluid_of(building_ref)
    place = lax.axis_index("gx")
    quarter = near_ref.shape[0]
    zero = jnp.zeros((SUB, LANE), jnp.float32)
    preceding, following = [zero, zero], [zero, zero]
    ghost_prev, ghost_next = preceding, following
    for ref, at in (
        (half_ref, place // (2 * quarter)), (pair_ref, place // quarter % 2), (near_ref, place % quarter)
    ):
        main, extra = blocks_of(ref)
        preceding, following = interface(main, at, preceding, following)
        ghost_prev, ghost_next = interface(extra, at, ghost_prev, ghost_next)
    ghosts = []
    for s in range(2):
        ghosts.append(
            [
                ghost_ref[4 * s + h]
                + ghost_ref[4 * s + 2] * ghost_prev[h][:, s : s + 1]
                + ghost_ref[4 * s + 3] * ghost_next[h][:, s : s + 1]
                for h in range(2)
            ]
        )
    quads = [edge_quads(ghosts[0][h], ghosts[1][h]) for h in range(2)]

    def rows(step, after):
        k = 15 - step
        for n in reversed(range(8)):
            row = 8 * k + n
            ratio, from_prev = push * kept_ref[row, INV], kept_ref[row, FROM_PREV]
            west, east = kept_ref[row, WEST], kept_ref[row, EAST]
            near, near_low, near_up = kept_ref[row, NEAR], kept_ref[row, NEAR_LOW], kept_ref[row, NEAR_UP]
            far, far_low, far_up = kept_ref[row, FAR], kept_ref[row, FAR_LOW], kept_ref[row, FAR_UP]
            centre = 2.0 - west - east
            new_after = []
            for h in range(2):
                at = slice(8 * h, 8 * h + 8)
                star = (partial_ref[row, at, :] + from_prev * preceding[h]) + ratio * after[h]
                left, right = neighbours(star, quads[h], (8 * k, n))
                side = (centre * star - side_ref[row, at, :]) + (west * left + east * right)
                value = near * side + near_low * subs(side, 1) + near_up * subs(side, -1)
                out_ref[row, at, :] = far * value + far_low * subs(value, 2) + far_up * subs(value, -2)
                new_after.append(star)
            after = new_after
        written(k).start()
        return after

    def written(k):
        return pltpu.make_async_copy(out_ref.at[pl.ds(8 * k, 8)], out_hbm.at[pl.ds(8 * k, 8)], sems.at[k])

    lax.fori_loop(0, 16, rows, following)
    for k in range(16):
        written(k).wait()


def call(kernel, out_shapes, in_specs, flops, bytes_accessed, limit=LIMIT, scratch=(), out_space=VMEM):
    return pl.pallas_call(
        kernel,
        out_shape=[jax.ShapeDtypeStruct(shape, jnp.float32) for shape in out_shapes],
        in_specs=in_specs,
        out_specs=[out_space] * len(out_shapes),
        scratch_shapes=list(scratch),
        compiler_params=pltpu.CompilerParams(vmem_limit_bytes=limit),
        cost_estimate=pl.CostEstimate(flops=flops, bytes_accessed=bytes_accessed, transcendentals=0),
    )


def on_device(concentration, courant_x, courant_y, vert_diff, emission, building):
    cells, tracers, levels, span = concentration.shape
    blocks = lax.axis_size("gx")
    devices = lax.axis_size("gy")
    c = concentration.reshape(cells, tracers * levels, span)
    coefs = [x.reshape(cells // 2, 2 * levels, span) for x in (courant_x, courant_y, vert_diff, emission)]
    field = (cells, 2 * SUB, LANE)
    packed = (6, SUB, LANE)
    sent_a, sent_b, c, cx, cy, vd, em = call(
        pack_kernel,
        [packed, packed, field] + [x.shape for x in coefs],
        [HBM] * 5 + [SMEM],
        10**6,
        2 * 10**6,
        scratch=[pltpu.SemaphoreType.DMA((CHUNKS + 4,))],
    )(*(pltpu.with_memory_space_constraint(x, pltpu.HBM) for x in (c, *coefs)), building)
    pairs_a = [(i, i + 1) for i in range(0, devices, 2)]
    pairs_b = [(i, (i + 1) % devices) for i in range(1, devices, 2)]
    got_b = lax.ppermute(sent_b, "gy", pairs_b + [(b, a) for a, b in pairs_b])
    got_a = lax.ppermute(sent_a, "gy", pairs_a + [(b, a) for a, b in pairs_a])
    kept, ends = call(
        factor_kernel, [(cells, KEPT, SUB, LANE), (2, SUB, LANE)], [VMEM] * 3 + [SMEM], 10**7, 10**7
    )(cx, cy, vd, building)
    side, partial, ghost, mine = call(
        side_kernel, [field, field, (8, SUB, LANE), (7, SUB, LANE)], [VMEM] * 4 + [SMEM] + [VMEM] * 4, 10**7, 10**7
    )(c, em, kept, ends, building, sent_b, sent_a, got_b, got_a)
    quarter = blocks // 4
    near_groups = [[q * quarter + i for i in range(quarter)] for q in range(4)]
    pair_groups = [[q * quarter + i, (q + 1) * quarter + i] for q in (0, 2) for i in range(quarter)]
    half_groups = [[q * quarter + i, r * quarter + i] for q, r in ((1, 2), (0, 3)) for i in range(quarter)]
    near = lax.all_gather(mine, "gx", axis_index_groups=near_groups)
    (mine,) = call(condense_kernel, [mine.shape], [VMEM], 10**5, 10**5)(near)
    pair = lax.all_gather(mine, "gx", axis_index_groups=pair_groups)
    (mine,) = call(condense_kernel, [mine.shape], [VMEM], 10**5, 10**5)(pair)
    half = lax.all_gather(mine, "gx", axis_index_groups=half_groups)
    (updated,) = call(
        finish_kernel,
        [field],
        [VMEM] * 7 + [SMEM],
        10**7,
        10**7,
        scratch=[pltpu.VMEM(field, jnp.float32), pltpu.SemaphoreType.DMA((16,))],
        out_space=HBM,
    )(side, partial, kept, ghost, near, pair, half, building)
    return updated.reshape(concentration.shape)


def solution(mesh):
    in_specs = (
        P("gx", None, None, "gy"),
        P("gx", None, "gy"),
        P("gx", None, "gy"),
        P("gx", None, "gy"),
        P("gx", None, "gy"),
        P("gx", "gy"),
    )
    return jax.shard_map(
        on_device, mesh=mesh, in_specs=in_specs, out_specs=P("gx", None, None, "gy"), check_vma=False
    )
```

```python
import functools

import jax
import jax.numpy as jnp
from jax import lax
from jax.experimental import pallas as pl
from jax.experimental.pallas import tpu as pltpu
from jax.sharding import PartitionSpec as P

cross_diff = 300.0
span_diff = 0.25

SUB, LANE = 8, 128
VMEM = pl.BlockSpec(memory_space=pltpu.VMEM)
HBM = pl.BlockSpec(memory_space=pltpu.HBM)
SMEM = pl.BlockSpec(memory_space=pltpu.SMEM)
LIMIT = 16 * 1024 * 1024
(INV, PULLED, FROM_PREV, WEST, EAST, CENTRE, BELOW, ABOVE, NEAR, NEAR_LOW, NEAR_UP, FAR, FAR_LOW, FAR_UP) = range(14)
KEPT = 14
CHUNKS = 2
PEEL = 16
PEEL_FACTOR = 16
PEEL_FINISH = 16


def sub_ids():
    return lax.broadcasted_iota(jnp.int32, (SUB, LANE), 0)


def lane_ids():
    return lax.broadcasted_iota(jnp.int32, (SUB, LANE), 1)


def lanes(x, shift):
    shift %= LANE
    return pltpu.roll(x, shift, 1) if shift else x


def subs(x, shift):
    shift %= SUB
    return pltpu.roll(x, shift, 0) if shift else x


def stepped(body, state, peeled):
    for k in range(peeled):
        state = body(k, state)
    return lax.fori_loop(peeled, 16, body, state) if peeled < 16 else state


def fluid_of(building_ref):
    return 1.0 - building_ref[0, 0].astype(jnp.float32)


def both_rows(pair):
    low = sub_ids() < 4
    turned = subs(pair, 4)
    return jnp.where(low, pair, turned), jnp.where(low, turned, pair)


def level_above(x):
    return jnp.where(sub_ids() % 4 == 3, 0.0, subs(x, -1))


def level_below(x):
    return jnp.where(sub_ids() % 4 == 0, 0.0, subs(x, 1))


def edge_quads(west, east):
    at_west = lane_ids() % 4 == 2
    return [jnp.where(at_west, lanes(west, 2 - g), lanes(east, 1 - g)) for g in range(4)]


def neighbours(q, quads, row):
    base, offset = row
    turn = 126 - base - offset // 4 * 4
    edge = pltpu.roll(quads[offset % 4], turn, 1)
    lane = lane_ids()
    return jnp.where(lane == 0, edge, lanes(q, 1)), jnp.where(lane == LANE - 1, edge, lanes(q, -1))


def pack_kernel(
    c_hbm, cx_hbm, cy_hbm, vd_hbm, em_hbm, building_ref,
    a_ref, b_ref, c_ref, cx_ref, cy_ref, vd_ref, em_ref, sems,
):
    coefs = ((cx_hbm, cx_ref), (cy_hbm, cy_ref), (vd_hbm, vd_ref), (em_hbm, em_ref))
    size = c_ref.shape[0] // CHUNKS
    copies = [
        pltpu.make_async_copy(c_hbm.at[pl.ds(n * size, size)], c_ref.at[pl.ds(n * size, size)], sems.at[n])
        for n in range(CHUNKS)
    ]
    copies += [pltpu.make_async_copy(src, dst, sems.at[CHUNKS + n]) for n, (src, dst) in enumerate(coefs)]
    for copy in copies:
        copy.start()

    lane, sub = lane_ids(), sub_ids()
    fluid = fluid_of(building_ref)
    low = sub < 4
    even_gy = lax.rem(lax.axis_index("gy"), 2) == 0
    quarter = lane // 4
    zero = jnp.zeros((SUB, LANE), jnp.float32)
    picked = [[zero] * 4 for _ in range(2)]
    for n in range(CHUNKS):
        copies[n].wait()
        for m in range(n * size // 4, (n + 1) * size // 4):
            here = quarter == m
            for g in range(4):
                for half in range(2):
                    turned = lanes(c_ref[4 * m + g, 8 * half : 8 * half + 8, :], 4 * m + 2)
                    picked[half][g] = jnp.where(here, turned, picked[half][g])
    columns = []
    for half in range(2):
        found = []
        for j in range(4):
            out = lanes(picked[half][0], -j)
            for g in range(1, 4):
                out = jnp.where(lane % 4 == g, lanes(picked[half][g], g - j), out)
            found.append(out)
        columns.append(found)
    even = lane % 2 == 0
    pair_of = lane // 2
    first, last = [], []
    for n, (_, ref) in enumerate(coefs):
        copies[CHUNKS + n].wait()
        acc = zero
        for k in range(64):
            acc = jnp.where(pair_of == k, lanes(ref[k], 2 * k + 1), acc)
        turned = subs(acc, 4)
        at_even = jnp.where(low, acc, turned)
        at_odd = jnp.where(low, turned, acc)
        last.append(jnp.where(even, at_even, lanes(at_odd, 1)))
        first.append(jnp.where(even, lanes(at_even, -1), at_odd))
    sides = []
    for (outer, inner), edge in (((2, 3), first), ((1, 0), last)):
        pull = fluid * (edge[0] + cross_diff)
        sides.append(
            [
                columns[0][outer],
                columns[1][outer],
                columns[0][inner],
                columns[1][inner],
                jnp.where(low, pull, edge[1]),
                jnp.where(low, edge[2], edge[3]),
            ]
        )
    for n in range(6):
        to_left, to_right = sides[0][n], sides[1][n]
        a_ref[n] = jnp.where(even_gy, to_right, to_left)
        b_ref[n] = jnp.where(even_gy, to_left, to_right)


def factor_kernel(cx_ref, cy_ref, vd_ref, building_ref, kept_ref, ends_ref):
    fluid = fluid_of(building_ref)
    push = cross_diff * fluid
    ground = sub_ids() % 4 == 0

    def rows(k, state):
        ratio, from_prev, chain, first_prev = state
        for u in range(4):
            pair = 4 * k + u
            wind, face = cy_ref[pair], vd_ref[pair]
            face_up = level_above(face)
            west = fluid * (jnp.maximum(wind, 0.0) + span_diff)
            east = fluid * (jnp.maximum(-wind, 0.0) + span_diff)
            inv = 1.0 / (1.0 + face + face_up)
            lower = jnp.where(ground, 0.0, face * inv)
            upper = face_up * inv
            near = 1.0 / (1.0 - lower * subs(upper, 1) - upper * subs(lower, -1))
            near_low, near_up = near * lower, near * upper
            far_low, far_up = near_low * subs(lower, 1), near_up * subs(upper, -1)
            far = 1.0 / (1.0 - far_low * subs(far_up, 2) - far_up * subs(far_low, -2))
            scale = fluid * inv
            pairs = {
                WEST: west,
                EAST: east,
                CENTRE: fluid * (1.0 - face - face_up) - west - east,
                BELOW: jnp.where(ground, 0.0, fluid * face),
                ABOVE: fluid * face_up,
                NEAR: near * scale,
                NEAR_LOW: near_low * subs(scale, 1),
                NEAR_UP: near_up * subs(scale, -1),
                FAR: far,
                FAR_LOW: far * far_low,
                FAR_UP: far * far_up,
            }
            for n, value in pairs.items():
                kept_ref[2 * pair, n], kept_ref[2 * pair + 1, n] = both_rows(value)
            for r, pull in enumerate(both_rows(fluid * (cx_ref[pair] + cross_diff))):
                row = 2 * pair + r
                inv = 1.0 / ((1.0 + pull + push) - pull * ratio)
                pulled = pull * inv
                from_prev = pulled * from_prev
                first_prev = first_prev + chain * from_prev
                ratio = push * inv
                chain = chain * ratio
                kept_ref[row, INV] = inv
                kept_ref[row, PULLED] = pulled
                kept_ref[row, FROM_PREV] = from_prev
        return ratio, from_prev, chain, first_prev

    zero = jnp.zeros((SUB, LANE), jnp.float32)
    ratio, from_prev, chain, first_prev = stepped(
        rows, (zero, zero + 1.0, zero + 1.0, zero), PEEL_FACTOR
    )
    low = sub_ids() < 4
    ends_ref[0] = jnp.where(low, first_prev, chain)
    ends_ref[1] = jnp.where(low, from_prev, ratio)


def merge(left, right, part):
    low = sub_ids() < 4
    return jnp.where(low, left, subs(right, 4)) if part == 0 else jnp.where(low, subs(left, 4), right)


def ghost_columns(from_left, from_right, own_left, own_right):
    lane, sub = lane_ids(), sub_ids()
    pull, wind = merge(from_left[4], from_right[4], 0), merge(from_left[4], from_right[4], 1)
    face, emitted = merge(from_left[5], from_right[5], 0), merge(from_left[5], from_right[5], 1)
    fluid = jnp.where(pull > 0.0, 1.0, 0.0)
    face_up = level_above(face)
    west = jnp.maximum(wind, 0.0) + span_diff
    east = jnp.maximum(-wind, 0.0) + span_diff
    inv = 1.0 / (1.0 + pull + cross_diff * fluid)
    lower = pull * inv
    upper = cross_diff * fluid * inv
    sides = []
    for t in range(4):
        h, part = t // 2, t % 2
        q = merge(from_left[h], from_right[h], part)
        left = merge(from_left[2 + h], own_right[h], part)
        right = merge(own_left[h], from_right[2 + h], part)
        side = q + west * (left - q) + east * (right - q)
        side = side + face * (level_below(q) - q) + face_up * (level_above(q) - q)
        side = side + jnp.where(sub % 4 == 0, subs(emitted, -t), 0.0)
        sides.append(inv * fluid * side)
    sides.append(jnp.where(lane == 0, lower, 0.0))
    sides.append(jnp.where(lane == LANE - 1, upper, 0.0))
    lower = jnp.where(lane == 0, 0.0, lower)
    upper = jnp.where(lane == LANE - 1, 0.0, upper)
    step = 1
    while step < LANE:
        low_prev, up_prev = lanes(lower, step), lanes(upper, step)
        low_next, up_next = lanes(lower, -step), lanes(upper, -step)
        inv = 1.0 / (1.0 - lower * up_prev - upper * low_next)
        from_low, from_up = inv * lower, inv * upper
        sides = [inv * s + from_low * lanes(s, step) + from_up * lanes(s, -step) for s in sides]
        lower, upper = from_low * low_prev, from_up * up_next
        step *= 2
    prev, following = both_rows(sides[4]), both_rows(sides[5])
    return [
        [merge(sides[0], sides[1], s), merge(sides[2], sides[3], s), prev[s], following[s]] for s in range(2)
    ]


def side_kernel(
    c_ref, em_ref, kept_ref, ends_ref, building_ref, sent_a_ref, sent_b_ref, got_a_ref, got_b_ref,
    side_ref, partial_ref, ghost_ref, rows_ref,
):
    lane, sub = lane_ids(), sub_ids()
    fluid = fluid_of(building_ref)
    push = cross_diff * fluid
    even_gy = lax.rem(lax.axis_index("gy"), 2) == 0
    own_left = [jnp.where(even_gy, sent_b_ref[n], sent_a_ref[n]) for n in range(2)]
    own_right = [jnp.where(even_gy, sent_a_ref[n], sent_b_ref[n]) for n in range(2)]
    from_left = [jnp.where(even_gy, got_b_ref[n], got_a_ref[n]) for n in range(6)]
    from_right = [jnp.where(even_gy, got_a_ref[n], got_b_ref[n]) for n in range(6)]

    extra = jnp.zeros((SUB, LANE), jnp.float32)
    for s, parts in enumerate(ghost_columns(from_left, from_right, own_left, own_right)):
        for n in range(4):
            ghost_ref[4 * s + n] = parts[n]
        ends = [
            (parts[0], 0), (parts[1], 0), (parts[0], 1), (parts[1], 1),
            (parts[2], 0), (parts[3], 0), (parts[2], 1), (parts[3], 1),
        ]
        for j, (part, tail) in enumerate(ends):
            extra = jnp.where(lane == 2 * j + s, lanes(part, 2 * j + s + tail), extra)

    quads = [edge_quads(from_left[h], from_right[h]) for h in range(2)]

    def rows(k, state):
        last, first, chain = state
        for n in range(8):
            row, pair = 8 * k + n, 4 * k + n // 2
            inv, pulled = kept_ref[row, INV], kept_ref[row, PULLED]
            west, east, centre = kept_ref[row, WEST], kept_ref[row, EAST], kept_ref[row, CENTRE]
            below, above = kept_ref[row, BELOW], kept_ref[row, ABOVE]
            new_last, new_first = [], []
            for h in range(2):
                q = c_ref[row, 8 * h : 8 * h + 8, :]
                left, right = neighbours(q, quads[h], (8 * k, n))
                tracer = 4 * (n % 2) + 2 * h
                source = jnp.where(
                    sub == 0,
                    em_ref[pair, tracer : tracer + 1, :],
                    jnp.where(sub == 4, em_ref[pair, tracer + 1 : tracer + 2, :], 0.0),
                )
                side = (centre * q + fluid * source) + (west * left + east * right)
                side = side + (below * subs(q, 1) + above * subs(q, -1))
                value = side * inv + pulled * last[h]
                side_ref[row, 8 * h : 8 * h + 8, :] = side
                partial_ref[row, 8 * h : 8 * h + 8, :] = value
                new_last.append(value)
                new_first.append(first[h] + chain * value)
            last, first = new_last, new_first
            chain = chain * (push * inv)
        return last, first, chain

    zero = jnp.zeros((SUB, LANE), jnp.float32)
    state = ([zero, zero], [zero, zero], zero + 1.0)
    last, first, _ = stepped(rows, state, PEEL)
    rows_ref[0], rows_ref[1] = first
    rows_ref[2], rows_ref[3] = last
    rows_ref[4] = ends_ref[0]
    rows_ref[5] = ends_ref[1]
    rows_ref[6] = extra


def blocks_of(rows_ref):
    main, extra = [], []
    for k in range(rows_ref.shape[0]):
        first_prev, first_next = both_rows(rows_ref[k, 4])
        last_prev, last_next = both_rows(rows_ref[k, 5])
        main.append(
            ([rows_ref[k, 0], rows_ref[k, 1]], [rows_ref[k, 2], rows_ref[k, 3]],
             first_prev, first_next, last_prev, last_next)
        )
        e = [lanes(rows_ref[k, 6], -2 * j) for j in range(8)]
        extra.append((e[0:2], e[2:4], e[4], e[5], e[6], e[7]))
    return main, extra


def joined(before, after):
    first, last, first_prev, first_next, last_prev, last_next = before
    first_b, last_b, first_prev_b, first_next_b, last_prev_b, last_next_b = after
    inv = 1.0 / (1.0 - last_next * first_prev_b)
    low_own = [(last[h] + last_next * first_b[h]) * inv for h in range(2)]
    low_prev, low_next = last_prev * inv, last_next * first_next_b * inv
    high_own = [first_b[h] + first_prev_b * low_own[h] for h in range(2)]
    high_prev, high_next = first_prev_b * low_prev, first_next_b + first_prev_b * low_next
    return (
        [first[h] + first_next * high_own[h] for h in range(2)],
        [last_b[h] + last_prev_b * low_own[h] for h in range(2)],
        first_prev + first_next * high_prev,
        first_next * high_next,
        last_prev_b * low_prev,
        last_next_b + last_prev_b * low_next,
    )


def condense_kernel(rows_ref, out_ref):
    main, extra = (functools.reduce(joined, forms) for forms in blocks_of(rows_ref))
    low, lane = sub_ids() < 4, lane_ids()
    out_ref[0], out_ref[1] = main[0]
    out_ref[2], out_ref[3] = main[1]
    out_ref[4] = jnp.where(low, main[2], main[3])
    out_ref[5] = jnp.where(low, main[4], main[5])
    packed = extra[0][0]
    for j, part in enumerate((extra[0][1], *extra[1], *extra[2:]), 1):
        packed = jnp.where(lane // 2 == j, lanes(part, 2 * j), packed)
    out_ref[6] = packed


def interface(blocks, place, before, beyond):
    zero = jnp.zeros((SUB, LANE), jnp.float32)
    own, slope = before, zero
    kept_own, kept_slope = own, slope
    forms = []
    for k, (first, last, first_prev, first_next, last_prev, last_next) in enumerate(blocks):
        if k:
            here = place == k
            kept_own = [jnp.where(here, own[h], kept_own[h]) for h in range(2)]
            kept_slope = jnp.where(here, slope, kept_slope)
        inv = 1.0 / (1.0 - first_prev * slope)
        start = [(first[h] + first_prev * own[h]) * inv for h in range(2)]
        start_next = first_next * inv
        forms.append((start, start_next))
        carried = last_prev * slope
        own = [last[h] + last_prev * own[h] + carried * start[h] for h in range(2)]
        slope = last_next + carried * start_next
    after = beyond
    following, mine = after, after
    for k in reversed(range(len(forms))):
        following = [jnp.where(place == k, after[h], following[h]) for h in range(2)]
        start, start_next = forms[k]
        after = [start[h] + start_next * after[h] for h in range(2)]
        mine = [jnp.where(place == k, after[h], mine[h]) for h in range(2)]
    preceding = [kept_own[h] + kept_slope * mine[h] for h in range(2)]
    return preceding, following


def finish_kernel(
    side_ref, partial_ref, kept_ref, ghost_ref, near_ref, pair_ref, half_ref, building_ref, out_hbm, out_ref, sems
):
    push = cross_diff * fluid_of(building_ref)
    place = lax.axis_index("gx")
    quarter = near_ref.shape[0]
    zero = jnp.zeros((SUB, LANE), jnp.float32)
    preceding, following = [zero, zero], [zero, zero]
    ghost_prev, ghost_next = preceding, following
    for ref, at in (
        (half_ref, place // (2 * quarter)), (pair_ref, place // quarter % 2), (near_ref, place % quarter)
    ):
        main, extra = blocks_of(ref)
        preceding, following = interface(main, at, preceding, following)
        ghost_prev, ghost_next = interface(extra, at, ghost_prev, ghost_next)
    ghosts = []
    for s in range(2):
        ghosts.append(
            [
                ghost_ref[4 * s + h]
                + ghost_ref[4 * s + 2] * ghost_prev[h][:, s : s + 1]
                + ghost_ref[4 * s + 3] * ghost_next[h][:, s : s + 1]
                for h in range(2)
            ]
        )
    quads = [edge_quads(ghosts[0][h], ghosts[1][h]) for h in range(2)]

    def rows(step, after):
        k = 15 - step
        for n in reversed(range(8)):
            row = 8 * k + n
            ratio, from_prev = push * kept_ref[row, INV], kept_ref[row, FROM_PREV]
            west, east = kept_ref[row, WEST], kept_ref[row, EAST]
            near, near_low, near_up = kept_ref[row, NEAR], kept_ref[row, NEAR_LOW], kept_ref[row, NEAR_UP]
            far, far_low, far_up = kept_ref[row, FAR], kept_ref[row, FAR_LOW], kept_ref[row, FAR_UP]
            centre = 2.0 - west - east
            new_after = []
            for h in range(2):
                at = slice(8 * h, 8 * h + 8)
                star = (partial_ref[row, at, :] + from_prev * preceding[h]) + ratio * after[h]
                left, right = neighbours(star, quads[h], (8 * k, n))
                side = (centre * star - side_ref[row, at, :]) + (west * left + east * right)
                value = near * side + near_low * subs(side, 1) + near_up * subs(side, -1)
                out_ref[row, at, :] = far * value + far_low * subs(value, 2) + far_up * subs(value, -2)
                new_after.append(star)
            after = new_after
        written(k).start()
        return after

    def written(k):
        return pltpu.make_async_copy(out_ref.at[pl.ds(8 * k, 8)], out_hbm.at[pl.ds(8 * k, 8)], sems.at[k])

    stepped(rows, following, PEEL_FINISH)
    for k in range(16):
        written(k).wait()


def call(kernel, out_shapes, in_specs, flops, bytes_accessed, limit=LIMIT, scratch=(), out_space=VMEM):
    return pl.pallas_call(
        kernel,
        out_shape=[jax.ShapeDtypeStruct(shape, jnp.float32) for shape in out_shapes],
        in_specs=in_specs,
        out_specs=[out_space] * len(out_shapes),
        scratch_shapes=list(scratch),
        compiler_params=pltpu.CompilerParams(vmem_limit_bytes=limit),
        cost_estimate=pl.CostEstimate(flops=flops, bytes_accessed=bytes_accessed, transcendentals=0),
    )


def on_device(concentration, courant_x, courant_y, vert_diff, emission, building):
    cells, tracers, levels, span = concentration.shape
    blocks = lax.axis_size("gx")
    devices = lax.axis_size("gy")
    c = concentration.reshape(cells, tracers * levels, span)
    coefs = [x.reshape(cells // 2, 2 * levels, span) for x in (courant_x, courant_y, vert_diff, emission)]
    field = (cells, 2 * SUB, LANE)
    packed = (6, SUB, LANE)
    sent_a, sent_b, c, cx, cy, vd, em = call(
        pack_kernel,
        [packed, packed, field] + [x.shape for x in coefs],
        [HBM] * 5 + [SMEM],
        10**6,
        2 * 10**6,
        scratch=[pltpu.SemaphoreType.DMA((CHUNKS + 4,))],
    )(*(pltpu.with_memory_space_constraint(x, pltpu.HBM) for x in (c, *coefs)), building)
    pairs_a = [(i, i + 1) for i in range(0, devices, 2)]
    pairs_b = [(i, (i + 1) % devices) for i in range(1, devices, 2)]
    got_a = lax.ppermute(sent_a, "gy", pairs_a + [(b, a) for a, b in pairs_a])
    got_b = lax.ppermute(sent_b, "gy", pairs_b + [(b, a) for a, b in pairs_b])
    kept, ends = call(
        factor_kernel, [(cells, KEPT, SUB, LANE), (2, SUB, LANE)], [VMEM] * 3 + [SMEM], 10**7, 10**7
    )(cx, cy, vd, building)
    side, partial, ghost, mine = call(
        side_kernel, [field, field, (8, SUB, LANE), (7, SUB, LANE)], [VMEM] * 4 + [SMEM] + [VMEM] * 4, 10**7, 10**7
    )(c, em, kept, ends, building, sent_a, sent_b, got_a, got_b)
    quarter = blocks // 4
    near_groups = [[q * quarter + i for i in range(quarter)] for q in range(4)]
    pair_groups = [[q * quarter + i, (q + 1) * quarter + i] for q in (0, 2) for i in range(quarter)]
    half_groups = [[q * quarter + i, r * quarter + i] for q, r in ((1, 2), (0, 3)) for i in range(quarter)]
    near = lax.all_gather(mine, "gx", axis_index_groups=near_groups)
    (mine,) = call(condense_kernel, [mine.shape], [VMEM], 10**5, 10**5)(near)
    pair = lax.all_gather(mine, "gx", axis_index_groups=pair_groups)
    (mine,) = call(condense_kernel, [mine.shape], [VMEM], 10**5, 10**5)(pair)
    half = lax.all_gather(mine, "gx", axis_index_groups=half_groups)
    (updated,) = call(
        finish_kernel,
        [field],
        [VMEM] * 7 + [SMEM],
        10**7,
        10**7,
        scratch=[pltpu.VMEM(field, jnp.float32), pltpu.SemaphoreType.DMA((16,))],
        out_space=HBM,
    )(side, partial, kept, ghost, near, pair, half, building)
    return updated.reshape(concentration.shape)


def solution(mesh):
    in_specs = (
        P("gx", None, None, "gy"),
        P("gx", None, "gy"),
        P("gx", None, "gy"),
        P("gx", None, "gy"),
        P("gx", None, "gy"),
        P("gx", "gy"),
    )
    return jax.shard_map(
        on_device, mesh=mesh, in_specs=in_specs, out_specs=P("gx", None, None, "gy"), check_vma=False
    )
```

```python
import functools

import jax
import jax.numpy as jnp
from jax import lax
from jax.experimental import pallas as pl
from jax.experimental.pallas import tpu as pltpu
from jax.sharding import PartitionSpec as P

cross_diff = 300.0
span_diff = 0.25

SUB, LANE = 8, 128
VMEM = pl.BlockSpec(memory_space=pltpu.VMEM)
HBM = pl.BlockSpec(memory_space=pltpu.HBM)
ANY = pl.BlockSpec(memory_space=pl.ANY)
SMEM = pl.BlockSpec(memory_space=pltpu.SMEM)
LIMIT = 16 * 1024 * 1024
(INV, PULLED, FROM_PREV, WEST, EAST, CENTRE, BELOW, ABOVE, NEAR, NEAR_LOW, NEAR_UP, FAR, FAR_LOW, FAR_UP) = range(14)
KEPT = 14
CHUNKS = 2
PEEL = 16
PEEL_FACTOR = 16
PEEL_FINISH = 16


def sub_ids():
    return lax.broadcasted_iota(jnp.int32, (SUB, LANE), 0)


def lane_ids():
    return lax.broadcasted_iota(jnp.int32, (SUB, LANE), 1)


def lanes(x, shift):
    shift %= LANE
    return pltpu.roll(x, shift, 1) if shift else x


def subs(x, shift):
    shift %= SUB
    return pltpu.roll(x, shift, 0) if shift else x


def stepped(body, state, peeled):
    for k in range(peeled):
        state = body(k, state)
    return lax.fori_loop(peeled, 16, body, state) if peeled < 16 else state


def fluid_of(building_ref):
    return 1.0 - building_ref[0, 0].astype(jnp.float32)


def both_rows(pair):
    low = sub_ids() < 4
    turned = subs(pair, 4)
    return jnp.where(low, pair, turned), jnp.where(low, turned, pair)


def level_above(x):
    return jnp.where(sub_ids() % 4 == 3, 0.0, subs(x, -1))


def level_below(x):
    return jnp.where(sub_ids() % 4 == 0, 0.0, subs(x, 1))


def edge_quads(west, east):
    at_west = lane_ids() % 4 == 2
    return [jnp.where(at_west, lanes(west, 2 - g), lanes(east, 1 - g)) for g in range(4)]


def neighbours(q, quads, row):
    base, offset = row
    turn = 126 - base - offset // 4 * 4
    edge = pltpu.roll(quads[offset % 4], turn, 1)
    lane = lane_ids()
    return jnp.where(lane == 0, edge, lanes(q, 1)), jnp.where(lane == LANE - 1, edge, lanes(q, -1))


def pack_kernel(
    c_hbm, cx_hbm, cy_hbm, vd_hbm, em_hbm, building_ref,
    a_ref, b_ref, c_ref, cx_ref, cy_ref, vd_ref, em_ref, sems,
):
    coefs = ((cx_hbm, cx_ref), (cy_hbm, cy_ref), (vd_hbm, vd_ref), (em_hbm, em_ref))
    size = c_ref.shape[0] // CHUNKS
    copies = [
        pltpu.make_async_copy(c_hbm.at[pl.ds(n * size, size)], c_ref.at[pl.ds(n * size, size)], sems.at[n])
        for n in range(CHUNKS)
    ]
    copies += [pltpu.make_async_copy(src, dst, sems.at[CHUNKS + n]) for n, (src, dst) in enumerate(coefs)]
    for copy in copies:
        copy.start()

    lane, sub = lane_ids(), sub_ids()
    fluid = fluid_of(building_ref)
    low = sub < 4
    even_gy = lax.rem(lax.axis_index("gy"), 2) == 0
    quarter = lane // 4
    zero = jnp.zeros((SUB, LANE), jnp.float32)
    picked = [[zero] * 4 for _ in range(2)]
    for n in range(CHUNKS):
        copies[n].wait()
        for m in range(n * size // 4, (n + 1) * size // 4):
            here = quarter == m
            for g in range(4):
                for half in range(2):
                    turned = lanes(c_ref[4 * m + g, 8 * half : 8 * half + 8, :], 4 * m + 2)
                    picked[half][g] = jnp.where(here, turned, picked[half][g])
    columns = []
    for half in range(2):
        found = []
        for j in range(4):
            out = lanes(picked[half][0], -j)
            for g in range(1, 4):
                out = jnp.where(lane % 4 == g, lanes(picked[half][g], g - j), out)
            found.append(out)
        columns.append(found)
    even = lane % 2 == 0
    pair_of = lane // 2
    first, last = [], []
    for n, (_, ref) in enumerate(coefs):
        copies[CHUNKS + n].wait()
        acc = zero
        for k in range(64):
            acc = jnp.where(pair_of == k, lanes(ref[k], 2 * k + 1), acc)
        turned = subs(acc, 4)
        at_even = jnp.where(low, acc, turned)
        at_odd = jnp.where(low, turned, acc)
        last.append(jnp.where(even, at_even, lanes(at_odd, 1)))
        first.append(jnp.where(even, lanes(at_even, -1), at_odd))
    sides = []
    for (outer, inner), edge in (((2, 3), first), ((1, 0), last)):
        pull = fluid * (edge[0] + cross_diff)
        sides.append(
            [
                columns[0][outer],
                columns[1][outer],
                columns[0][inner],
                columns[1][inner],
                jnp.where(low, pull, edge[1]),
                jnp.where(low, edge[2], edge[3]),
            ]
        )
    for n in range(6):
        to_left, to_right = sides[0][n], sides[1][n]
        a_ref[n] = jnp.where(even_gy, to_right, to_left)
        b_ref[n] = jnp.where(even_gy, to_left, to_right)


def factor_kernel(cx_ref, cy_ref, vd_ref, building_ref, early_ref, kept_ref, ends_ref):
    fluid = fluid_of(building_ref)
    push = cross_diff * fluid
    ground = sub_ids() % 4 == 0

    def rows(k, state):
        ratio, from_prev, chain, first_prev = state
        for u in range(4):
            pair = 4 * k + u
            wind, face = cy_ref[pair], vd_ref[pair]
            face_up = level_above(face)
            west = fluid * (jnp.maximum(wind, 0.0) + span_diff)
            east = fluid * (jnp.maximum(-wind, 0.0) + span_diff)
            inv = 1.0 / (1.0 + face + face_up)
            lower = jnp.where(ground, 0.0, face * inv)
            upper = face_up * inv
            near = 1.0 / (1.0 - lower * subs(upper, 1) - upper * subs(lower, -1))
            near_low, near_up = near * lower, near * upper
            far_low, far_up = near_low * subs(lower, 1), near_up * subs(upper, -1)
            far = 1.0 / (1.0 - far_low * subs(far_up, 2) - far_up * subs(far_low, -2))
            scale = fluid * inv
            pairs = {
                WEST: west,
                EAST: east,
                CENTRE: fluid * (1.0 - face - face_up) - west - east,
                BELOW: jnp.where(ground, 0.0, fluid * face),
                ABOVE: fluid * face_up,
                NEAR: near * scale,
                NEAR_LOW: near_low * subs(scale, 1),
                NEAR_UP: near_up * subs(scale, -1),
                FAR: far,
                FAR_LOW: far * far_low,
                FAR_UP: far * far_up,
            }
            for n, value in pairs.items():
                kept_ref[2 * pair, n], kept_ref[2 * pair + 1, n] = both_rows(value)
            for r, pull in enumerate(both_rows(fluid * (cx_ref[pair] + cross_diff))):
                row = 2 * pair + r
                inv = 1.0 / ((1.0 + pull + push) - pull * ratio)
                pulled = pull * inv
                from_prev = pulled * from_prev
                first_prev = first_prev + chain * from_prev
                ratio = push * inv
                chain = chain * ratio
                kept_ref[row, INV] = inv
                kept_ref[row, PULLED] = pulled
                kept_ref[row, FROM_PREV] = from_prev
        return ratio, from_prev, chain, first_prev

    zero = jnp.zeros((SUB, LANE), jnp.float32)
    ratio, from_prev, chain, first_prev = stepped(
        rows, (zero, zero + 1.0, zero + 1.0, zero), PEEL_FACTOR
    )
    low = sub_ids() < 4
    ends_ref[0] = jnp.where(low, first_prev, chain)
    ends_ref[1] = jnp.where(low, from_prev, ratio)


def merge(left, right, part):
    low = sub_ids() < 4
    return jnp.where(low, left, subs(right, 4)) if part == 0 else jnp.where(low, subs(left, 4), right)


def ghost_columns(from_left, from_right, own_left, own_right):
    lane, sub = lane_ids(), sub_ids()
    pull, wind = merge(from_left[4], from_right[4], 0), merge(from_left[4], from_right[4], 1)
    face, emitted = merge(from_left[5], from_right[5], 0), merge(from_left[5], from_right[5], 1)
    fluid = jnp.where(pull > 0.0, 1.0, 0.0)
    face_up = level_above(face)
    west = jnp.maximum(wind, 0.0) + span_diff
    east = jnp.maximum(-wind, 0.0) + span_diff
    inv = 1.0 / (1.0 + pull + cross_diff * fluid)
    lower = pull * inv
    upper = cross_diff * fluid * inv
    sides = []
    for t in range(4):
        h, part = t // 2, t % 2
        q = merge(from_left[h], from_right[h], part)
        left = merge(from_left[2 + h], own_right[h], part)
        right = merge(own_left[h], from_right[2 + h], part)
        side = q + west * (left - q) + east * (right - q)
        side = side + face * (level_below(q) - q) + face_up * (level_above(q) - q)
        side = side + jnp.where(sub % 4 == 0, subs(emitted, -t), 0.0)
        sides.append(inv * fluid * side)
    sides.append(jnp.where(lane == 0, lower, 0.0))
    sides.append(jnp.where(lane == LANE - 1, upper, 0.0))
    lower = jnp.where(lane == 0, 0.0, lower)
    upper = jnp.where(lane == LANE - 1, 0.0, upper)
    step = 1
    while step < LANE:
        low_prev, up_prev = lanes(lower, step), lanes(upper, step)
        low_next, up_next = lanes(lower, -step), lanes(upper, -step)
        inv = 1.0 / (1.0 - lower * up_prev - upper * low_next)
        from_low, from_up = inv * lower, inv * upper
        sides = [inv * s + from_low * lanes(s, step) + from_up * lanes(s, -step) for s in sides]
        lower, upper = from_low * low_prev, from_up * up_next
        step *= 2
    prev, following = both_rows(sides[4]), both_rows(sides[5])
    return [
        [merge(sides[0], sides[1], s), merge(sides[2], sides[3], s), prev[s], following[s]] for s in range(2)
    ]


def side_kernel(
    c_ref, em_ref, kept_ref, ends_ref, building_ref, sent_a_ref, sent_b_ref, got_early_ref, got_b_ref, got_late_ref,
    side_ref, partial_ref, ghost_ref, rows_ref,
):
    lane, sub = lane_ids(), sub_ids()
    fluid = fluid_of(building_ref)
    push = cross_diff * fluid
    even_gy = lax.rem(lax.axis_index("gy"), 2) == 0
    own_left = [jnp.where(even_gy, sent_b_ref[n], sent_a_ref[n]) for n in range(2)]
    own_right = [jnp.where(even_gy, sent_a_ref[n], sent_b_ref[n]) for n in range(2)]
    early = lax.axis_index("gy") < lax.axis_size("gy") // 4 * 2
    got_a = [jnp.where(early, got_early_ref[n], got_late_ref[n]) for n in range(6)]
    from_left = [jnp.where(even_gy, got_b_ref[n], got_a[n]) for n in range(6)]
    from_right = [jnp.where(even_gy, got_a[n], got_b_ref[n]) for n in range(6)]

    extra = jnp.zeros((SUB, LANE), jnp.float32)
    for s, parts in enumerate(ghost_columns(from_left, from_right, own_left, own_right)):
        for n in range(4):
            ghost_ref[4 * s + n] = parts[n]
        ends = [
            (parts[0], 0), (parts[1], 0), (parts[0], 1), (parts[1], 1),
            (parts[2], 0), (parts[3], 0), (parts[2], 1), (parts[3], 1),
        ]
        for j, (part, tail) in enumerate(ends):
            extra = jnp.where(lane == 2 * j + s, lanes(part, 2 * j + s + tail), extra)

    quads = [edge_quads(from_left[h], from_right[h]) for h in range(2)]

    def rows(k, state):
        last, first, chain = state
        for n in range(8):
            row, pair = 8 * k + n, 4 * k + n // 2
            inv, pulled = kept_ref[row, INV], kept_ref[row, PULLED]
            west, east, centre = kept_ref[row, WEST], kept_ref[row, EAST], kept_ref[row, CENTRE]
            below, above = kept_ref[row, BELOW], kept_ref[row, ABOVE]
            new_last, new_first = [], []
            for h in range(2):
                q = c_ref[row, 8 * h : 8 * h + 8, :]
                left, right = neighbours(q, quads[h], (8 * k, n))
                tracer = 4 * (n % 2) + 2 * h
                source = jnp.where(
                    sub == 0,
                    em_ref[pair, tracer : tracer + 1, :],
                    jnp.where(sub == 4, em_ref[pair, tracer + 1 : tracer + 2, :], 0.0),
                )
                side = (centre * q + fluid * source) + (west * left + east * right)
                side = side + (below * subs(q, 1) + above * subs(q, -1))
                value = side * inv + pulled * last[h]
                side_ref[row, 8 * h : 8 * h + 8, :] = side
                partial_ref[row, 8 * h : 8 * h + 8, :] = value
                new_last.append(value)
                new_first.append(first[h] + chain * value)
            last, first = new_last, new_first
            chain = chain * (push * inv)
        return last, first, chain

    zero = jnp.zeros((SUB, LANE), jnp.float32)
    state = ([zero, zero], [zero, zero], zero + 1.0)
    last, first, _ = stepped(rows, state, PEEL)
    rows_ref[0], rows_ref[1] = first
    rows_ref[2], rows_ref[3] = last
    rows_ref[4] = ends_ref[0]
    rows_ref[5] = ends_ref[1]
    rows_ref[6] = extra


def blocks_of(rows_ref):
    main, extra = [], []
    for k in range(rows_ref.shape[0]):
        first_prev, first_next = both_rows(rows_ref[k, 4])
        last_prev, last_next = both_rows(rows_ref[k, 5])
        main.append(
            ([rows_ref[k, 0], rows_ref[k, 1]], [rows_ref[k, 2], rows_ref[k, 3]],
             first_prev, first_next, last_prev, last_next)
        )
        e = [lanes(rows_ref[k, 6], -2 * j) for j in range(8)]
        extra.append((e[0:2], e[2:4], e[4], e[5], e[6], e[7]))
    return main, extra


def joined(before, after):
    first, last, first_prev, first_next, last_prev, last_next = before
    first_b, last_b, first_prev_b, first_next_b, last_prev_b, last_next_b = after
    inv = 1.0 / (1.0 - last_next * first_prev_b)
    low_own = [(last[h] + last_next * first_b[h]) * inv for h in range(2)]
    low_prev, low_next = last_prev * inv, last_next * first_next_b * inv
    high_own = [first_b[h] + first_prev_b * low_own[h] for h in range(2)]
    high_prev, high_next = first_prev_b * low_prev, first_next_b + first_prev_b * low_next
    return (
        [first[h] + first_next * high_own[h] for h in range(2)],
        [last_b[h] + last_prev_b * low_own[h] for h in range(2)],
        first_prev + first_next * high_prev,
        first_next * high_next,
        last_prev_b * low_prev,
        last_next_b + last_prev_b * low_next,
    )


def condense_kernel(rows_ref, out_ref):
    main, extra = (functools.reduce(joined, forms) for forms in blocks_of(rows_ref))
    low, lane = sub_ids() < 4, lane_ids()
    out_ref[0], out_ref[1] = main[0]
    out_ref[2], out_ref[3] = main[1]
    out_ref[4] = jnp.where(low, main[2], main[3])
    out_ref[5] = jnp.where(low, main[4], main[5])
    packed = extra[0][0]
    for j, part in enumerate((extra[0][1], *extra[1], *extra[2:]), 1):
        packed = jnp.where(lane // 2 == j, lanes(part, 2 * j), packed)
    out_ref[6] = packed


def interface(blocks, place, before, beyond):
    zero = jnp.zeros((SUB, LANE), jnp.float32)
    own, slope = before, zero
    kept_own, kept_slope = own, slope
    forms = []
    for k, (first, last, first_prev, first_next, last_prev, last_next) in enumerate(blocks):
        if k:
            here = place == k
            kept_own = [jnp.where(here, own[h], kept_own[h]) for h in range(2)]
            kept_slope = jnp.where(here, slope, kept_slope)
        inv = 1.0 / (1.0 - first_prev * slope)
        start = [(first[h] + first_prev * own[h]) * inv for h in range(2)]
        start_next = first_next * inv
        forms.append((start, start_next))
        carried = last_prev * slope
        own = [last[h] + last_prev * own[h] + carried * start[h] for h in range(2)]
        slope = last_next + carried * start_next
    after = beyond
    following, mine = after, after
    for k in reversed(range(len(forms))):
        following = [jnp.where(place == k, after[h], following[h]) for h in range(2)]
        start, start_next = forms[k]
        after = [start[h] + start_next * after[h] for h in range(2)]
        mine = [jnp.where(place == k, after[h], mine[h]) for h in range(2)]
    preceding = [kept_own[h] + kept_slope * mine[h] for h in range(2)]
    return preceding, following


def finish_kernel(
    side_ref, partial_ref, kept_ref, ghost_ref, near_ref, pair_ref, half_ref, building_ref, out_hbm, out_ref, sems
):
    push = cross_diff * fluid_of(building_ref)
    place = lax.axis_index("gx")
    quarter = near_ref.shape[0]
    zero = jnp.zeros((SUB, LANE), jnp.float32)
    preceding, following = [zero, zero], [zero, zero]
    ghost_prev, ghost_next = preceding, following
    for ref, at in (
        (half_ref, place // (2 * quarter)), (pair_ref, place // quarter % 2), (near_ref, place % quarter)
    ):
        main, extra = blocks_of(ref)
        preceding, following = interface(main, at, preceding, following)
        ghost_prev, ghost_next = interface(extra, at, ghost_prev, ghost_next)
    ghosts = []
    for s in range(2):
        ghosts.append(
            [
                ghost_ref[4 * s + h]
                + ghost_ref[4 * s + 2] * ghost_prev[h][:, s : s + 1]
                + ghost_ref[4 * s + 3] * ghost_next[h][:, s : s + 1]
                for h in range(2)
            ]
        )
    quads = [edge_quads(ghosts[0][h], ghosts[1][h]) for h in range(2)]

    def rows(step, after):
        k = 15 - step
        for n in reversed(range(8)):
            row = 8 * k + n
            ratio, from_prev = push * kept_ref[row, INV], kept_ref[row, FROM_PREV]
            west, east = kept_ref[row, WEST], kept_ref[row, EAST]
            near, near_low, near_up = kept_ref[row, NEAR], kept_ref[row, NEAR_LOW], kept_ref[row, NEAR_UP]
            far, far_low, far_up = kept_ref[row, FAR], kept_ref[row, FAR_LOW], kept_ref[row, FAR_UP]
            centre = 2.0 - west - east
            new_after = []
            for h in range(2):
                at = slice(8 * h, 8 * h + 8)
                star = (partial_ref[row, at, :] + from_prev * preceding[h]) + ratio * after[h]
                left, right = neighbours(star, quads[h], (8 * k, n))
                side = (centre * star - side_ref[row, at, :]) + (west * left + east * right)
                value = near * side + near_low * subs(side, 1) + near_up * subs(side, -1)
                out_ref[row, at, :] = far * value + far_low * subs(value, 2) + far_up * subs(value, -2)
                new_after.append(star)
            after = new_after
        written(k).start()
        return after

    def written(k):
        return pltpu.make_async_copy(out_ref.at[pl.ds(8 * k, 8)], out_hbm.at[pl.ds(8 * k, 8)], sems.at[k])

    stepped(rows, following, PEEL_FINISH)
    for k in range(16):
        written(k).wait()


def call(kernel, out_shapes, in_specs, flops, bytes_accessed, limit=LIMIT, scratch=(), out_space=VMEM):
    return pl.pallas_call(
        kernel,
        out_shape=[jax.ShapeDtypeStruct(shape, jnp.float32) for shape in out_shapes],
        in_specs=in_specs,
        out_specs=[out_space] * len(out_shapes),
        scratch_shapes=list(scratch),
        compiler_params=pltpu.CompilerParams(vmem_limit_bytes=limit),
        cost_estimate=pl.CostEstimate(flops=flops, bytes_accessed=bytes_accessed, transcendentals=0),
    )


def on_device(concentration, courant_x, courant_y, vert_diff, emission, building):
    cells, tracers, levels, span = concentration.shape
    blocks = lax.axis_size("gx")
    devices = lax.axis_size("gy")
    c = concentration.reshape(cells, tracers * levels, span)
    coefs = [x.reshape(cells // 2, 2 * levels, span) for x in (courant_x, courant_y, vert_diff, emission)]
    field = (cells, 2 * SUB, LANE)
    packed = (6, SUB, LANE)
    sent_a, sent_b, c, cx, cy, vd, em = call(
        pack_kernel,
        [packed, packed, field] + [x.shape for x in coefs],
        [HBM] * 5 + [SMEM],
        10**6,
        2 * 10**6,
        scratch=[pltpu.SemaphoreType.DMA((CHUNKS + 4,))],
    )(*(pltpu.with_memory_space_constraint(x, pltpu.HBM) for x in (c, *coefs)), building)
    half = devices // 4 * 2
    even = [(i, i + 1) for i in range(0, devices, 2)]
    odd = [(i, (i + 1) % devices) for i in range(1, devices, 2)]
    low, high = [p for p in even if p[0] < half], [p for p in even if p[0] >= half]
    got_early, got_b, got_late = (
        lax.ppermute(sent, "gy", pairs + [(b, a) for a, b in pairs])
        for sent, pairs in ((sent_a, low), (sent_b, odd), (sent_a, high))
    )
    kept, ends = call(
        factor_kernel, [(cells, KEPT, SUB, LANE), (2, SUB, LANE)], [VMEM] * 3 + [SMEM, ANY], 10**7, 10**7
    )(cx, cy, vd, building, got_early)
    side, partial, ghost, mine = call(
        side_kernel, [field, field, (8, SUB, LANE), (7, SUB, LANE)], [VMEM] * 4 + [SMEM] + [VMEM] * 5, 10**7, 10**7
    )(c, em, kept, ends, building, sent_a, sent_b, got_early, got_b, got_late)
    quarter = blocks // 4
    near_groups = [[q * quarter + i for i in range(quarter)] for q in range(4)]
    pair_groups = [[q * quarter + i, (q + 1) * quarter + i] for q in (0, 2) for i in range(quarter)]
    half_groups = [[q * quarter + i, r * quarter + i] for q, r in ((1, 2), (0, 3)) for i in range(quarter)]
    near = lax.all_gather(mine, "gx", axis_index_groups=near_groups)
    (mine,) = call(condense_kernel, [mine.shape], [VMEM], 10**5, 10**5)(near)
    pair = lax.all_gather(mine, "gx", axis_index_groups=pair_groups)
    (mine,) = call(condense_kernel, [mine.shape], [VMEM], 10**5, 10**5)(pair)
    half = lax.all_gather(mine, "gx", axis_index_groups=half_groups)
    (updated,) = call(
        finish_kernel,
        [field],
        [VMEM] * 7 + [SMEM],
        10**7,
        10**7,
        scratch=[pltpu.VMEM(field, jnp.float32), pltpu.SemaphoreType.DMA((16,))],
        out_space=HBM,
    )(side, partial, kept, ghost, near, pair, half, building)
    return updated.reshape(concentration.shape)


def solution(mesh):
    in_specs = (
        P("gx", None, None, "gy"),
        P("gx", None, "gy"),
        P("gx", None, "gy"),
        P("gx", None, "gy"),
        P("gx", None, "gy"),
        P("gx", "gy"),
    )
    return jax.shard_map(
        on_device, mesh=mesh, in_specs=in_specs, out_specs=P("gx", None, None, "gy"), check_vma=False
    )
```

```python
import functools

import jax
import jax.numpy as jnp
from jax import lax
from jax.experimental import pallas as pl
from jax.experimental.pallas import tpu as pltpu
from jax.sharding import PartitionSpec as P

cross_diff = 300.0
span_diff = 0.25

SUB, LANE = 8, 128
VMEM = pl.BlockSpec(memory_space=pltpu.VMEM)
HBM = pl.BlockSpec(memory_space=pltpu.HBM)
ANY = pl.BlockSpec(memory_space=pl.ANY)
SMEM = pl.BlockSpec(memory_space=pltpu.SMEM)
LIMIT = 16 * 1024 * 1024
(INV, PULLED, FROM_PREV, WEST, EAST, CENTRE, BELOW, ABOVE, NEAR, NEAR_LOW, NEAR_UP, FAR, FAR_LOW, FAR_UP) = range(14)
KEPT = 14
CHUNKS = 1
PEEL = 16
PEEL_FACTOR = 16
PEEL_FINISH = 16


def sub_ids():
    return lax.broadcasted_iota(jnp.int32, (SUB, LANE), 0)


def lane_ids():
    return lax.broadcasted_iota(jnp.int32, (SUB, LANE), 1)


def lanes(x, shift):
    shift %= LANE
    return pltpu.roll(x, shift, 1) if shift else x


def subs(x, shift):
    shift %= SUB
    return pltpu.roll(x, shift, 0) if shift else x


def stepped(body, state, peeled):
    for k in range(peeled):
        state = body(k, state)
    return lax.fori_loop(peeled, 16, body, state) if peeled < 16 else state


def fluid_of(building_ref):
    return 1.0 - building_ref[0, 0].astype(jnp.float32)


def both_rows(pair):
    low = sub_ids() < 4
    turned = subs(pair, 4)
    return jnp.where(low, pair, turned), jnp.where(low, turned, pair)


def level_above(x):
    return jnp.where(sub_ids() % 4 == 3, 0.0, subs(x, -1))


def level_below(x):
    return jnp.where(sub_ids() % 4 == 0, 0.0, subs(x, 1))


def edge_quads(west, east):
    at_west = lane_ids() % 4 == 2
    return [jnp.where(at_west, lanes(west, 2 - g), lanes(east, 1 - g)) for g in range(4)]


def neighbours(q, quads, row):
    base, offset = row
    turn = 126 - base - offset // 4 * 4
    edge = pltpu.roll(quads[offset % 4], turn, 1)
    lane = lane_ids()
    return jnp.where(lane == 0, edge, lanes(q, 1)), jnp.where(lane == LANE - 1, edge, lanes(q, -1))


def pack_kernel(
    c_hbm, cx_hbm, cy_hbm, vd_hbm, em_hbm, building_ref,
    a_ref, b_ref, c_ref, cx_ref, cy_ref, vd_ref, em_ref, sems,
):
    coefs = ((cx_hbm, cx_ref), (cy_hbm, cy_ref), (vd_hbm, vd_ref), (em_hbm, em_ref))
    size = c_ref.shape[0] // CHUNKS
    copies = [
        pltpu.make_async_copy(c_hbm.at[pl.ds(n * size, size)], c_ref.at[pl.ds(n * size, size)], sems.at[n])
        for n in range(CHUNKS)
    ]
    copies += [pltpu.make_async_copy(src, dst, sems.at[CHUNKS + n]) for n, (src, dst) in enumerate(coefs)]
    for copy in copies[CHUNKS:] + copies[:CHUNKS]:
        copy.start()

    lane, sub = lane_ids(), sub_ids()
    fluid = fluid_of(building_ref)
    low = sub < 4
    even_gy = lax.rem(lax.axis_index("gy"), 2) == 0
    quarter = lane // 4
    zero = jnp.zeros((SUB, LANE), jnp.float32)
    even = lane % 2 == 0
    pair_of = lane // 2
    first, last = [], []
    for n, (_, ref) in enumerate(coefs):
        copies[CHUNKS + n].wait()
        acc = zero
        for k in range(64):
            acc = jnp.where(pair_of == k, lanes(ref[k], 2 * k + 1), acc)
        turned = subs(acc, 4)
        at_even = jnp.where(low, acc, turned)
        at_odd = jnp.where(low, turned, acc)
        last.append(jnp.where(even, at_even, lanes(at_odd, 1)))
        first.append(jnp.where(even, lanes(at_even, -1), at_odd))
    picked = [[zero] * 4 for _ in range(2)]
    for n in range(CHUNKS):
        copies[n].wait()
        for m in range(n * size // 4, (n + 1) * size // 4):
            here = quarter == m
            for g in range(4):
                for half in range(2):
                    turned = lanes(c_ref[4 * m + g, 8 * half : 8 * half + 8, :], 4 * m + 2)
                    picked[half][g] = jnp.where(here, turned, picked[half][g])
    columns = []
    for half in range(2):
        found = []
        for j in range(4):
            out = lanes(picked[half][0], -j)
            for g in range(1, 4):
                out = jnp.where(lane % 4 == g, lanes(picked[half][g], g - j), out)
            found.append(out)
        columns.append(found)
    sides = []
    for (outer, inner), edge in (((2, 3), first), ((1, 0), last)):
        pull = fluid * (edge[0] + cross_diff)
        sides.append(
            [
                columns[0][outer],
                columns[1][outer],
                columns[0][inner],
                columns[1][inner],
                jnp.where(low, pull, edge[1]),
                jnp.where(low, edge[2], edge[3]),
            ]
        )
    for n in range(6):
        to_left, to_right = sides[0][n], sides[1][n]
        a_ref[n] = jnp.where(even_gy, to_right, to_left)
        b_ref[n] = jnp.where(even_gy, to_left, to_right)


def factor_kernel(cx_ref, cy_ref, vd_ref, building_ref, early_ref, kept_ref, ends_ref):
    fluid = fluid_of(building_ref)
    push = cross_diff * fluid
    ground = sub_ids() % 4 == 0

    def rows(k, state):
        ratio, from_prev, chain, first_prev = state
        for u in range(4):
            pair = 4 * k + u
            wind, face = cy_ref[pair], vd_ref[pair]
            face_up = level_above(face)
            west = fluid * (jnp.maximum(wind, 0.0) + span_diff)
            east = fluid * (jnp.maximum(-wind, 0.0) + span_diff)
            inv = 1.0 / (1.0 + face + face_up)
            lower = jnp.where(ground, 0.0, face * inv)
            upper = face_up * inv
            near = 1.0 / (1.0 - lower * subs(upper, 1) - upper * subs(lower, -1))
            near_low, near_up = near * lower, near * upper
            far_low, far_up = near_low * subs(lower, 1), near_up * subs(upper, -1)
            far = 1.0 / (1.0 - far_low * subs(far_up, 2) - far_up * subs(far_low, -2))
            scale = fluid * inv
            pairs = {
                WEST: west,
                EAST: east,
                CENTRE: fluid * (1.0 - face - face_up) - west - east,
                BELOW: jnp.where(ground, 0.0, fluid * face),
                ABOVE: fluid * face_up,
                NEAR: near * scale,
                NEAR_LOW: near_low * subs(scale, 1),
                NEAR_UP: near_up * subs(scale, -1),
                FAR: far,
                FAR_LOW: far * far_low,
                FAR_UP: far * far_up,
            }
            for n, value in pairs.items():
                kept_ref[2 * pair, n], kept_ref[2 * pair + 1, n] = both_rows(value)
            for r, pull in enumerate(both_rows(fluid * (cx_ref[pair] + cross_diff))):
                row = 2 * pair + r
                inv = 1.0 / ((1.0 + pull + push) - pull * ratio)
                pulled = pull * inv
                from_prev = pulled * from_prev
                first_prev = first_prev + chain * from_prev
                ratio = push * inv
                chain = chain * ratio
                kept_ref[row, INV] = inv
                kept_ref[row, PULLED] = pulled
                kept_ref[row, FROM_PREV] = from_prev
        return ratio, from_prev, chain, first_prev

    zero = jnp.zeros((SUB, LANE), jnp.float32)
    ratio, from_prev, chain, first_prev = stepped(
        rows, (zero, zero + 1.0, zero + 1.0, zero), PEEL_FACTOR
    )
    low = sub_ids() < 4
    ends_ref[0] = jnp.where(low, first_prev, chain)
    ends_ref[1] = jnp.where(low, from_prev, ratio)


def merge(left, right, part):
    low = sub_ids() < 4
    return jnp.where(low, left, subs(right, 4)) if part == 0 else jnp.where(low, subs(left, 4), right)


def ghost_columns(from_left, from_right, own_left, own_right):
    lane, sub = lane_ids(), sub_ids()
    pull, wind = merge(from_left[4], from_right[4], 0), merge(from_left[4], from_right[4], 1)
    face, emitted = merge(from_left[5], from_right[5], 0), merge(from_left[5], from_right[5], 1)
    fluid = jnp.where(pull > 0.0, 1.0, 0.0)
    face_up = level_above(face)
    west = jnp.maximum(wind, 0.0) + span_diff
    east = jnp.maximum(-wind, 0.0) + span_diff
    inv = 1.0 / (1.0 + pull + cross_diff * fluid)
    lower = pull * inv
    upper = cross_diff * fluid * inv
    sides = []
    for t in range(4):
        h, part = t // 2, t % 2
        q = merge(from_left[h], from_right[h], part)
        left = merge(from_left[2 + h], own_right[h], part)
        right = merge(own_left[h], from_right[2 + h], part)
        side = q + west * (left - q) + east * (right - q)
        side = side + face * (level_below(q) - q) + face_up * (level_above(q) - q)
        side = side + jnp.where(sub % 4 == 0, subs(emitted, -t), 0.0)
        sides.append(inv * fluid * side)
    sides.append(jnp.where(lane == 0, lower, 0.0))
    sides.append(jnp.where(lane == LANE - 1, upper, 0.0))
    lower = jnp.where(lane == 0, 0.0, lower)
    upper = jnp.where(lane == LANE - 1, 0.0, upper)
    step = 1
    while step < LANE:
        low_prev, up_prev = lanes(lower, step), lanes(upper, step)
        low_next, up_next = lanes(lower, -step), lanes(upper, -step)
        inv = 1.0 / (1.0 - lower * up_prev - upper * low_next)
        from_low, from_up = inv * lower, inv * upper
        sides = [inv * s + from_low * lanes(s, step) + from_up * lanes(s, -step) for s in sides]
        lower, upper = from_low * low_prev, from_up * up_next
        step *= 2
    prev, following = both_rows(sides[4]), both_rows(sides[5])
    return [
        [merge(sides[0], sides[1], s), merge(sides[2], sides[3], s), prev[s], following[s]] for s in range(2)
    ]


def side_kernel(
    c_ref, em_ref, kept_ref, ends_ref, building_ref, sent_a_ref, sent_b_ref, got_early_ref, got_b_ref, got_late_ref,
    side_ref, partial_ref, ghost_ref, rows_ref,
):
    lane, sub = lane_ids(), sub_ids()
    fluid = fluid_of(building_ref)
    push = cross_diff * fluid
    even_gy = lax.rem(lax.axis_index("gy"), 2) == 0
    own_left = [jnp.where(even_gy, sent_b_ref[n], sent_a_ref[n]) for n in range(2)]
    own_right = [jnp.where(even_gy, sent_a_ref[n], sent_b_ref[n]) for n in range(2)]
    early = lax.axis_index("gy") < lax.axis_size("gy") // 4 * 2
    got_a = [jnp.where(early, got_early_ref[n], got_late_ref[n]) for n in range(6)]
    from_left = [jnp.where(even_gy, got_b_ref[n], got_a[n]) for n in range(6)]
    from_right = [jnp.where(even_gy, got_a[n], got_b_ref[n]) for n in range(6)]

    extra = jnp.zeros((SUB, LANE), jnp.float32)
    for s, parts in enumerate(ghost_columns(from_left, from_right, own_left, own_right)):
        for n in range(4):
            ghost_ref[4 * s + n] = parts[n]
        ends = [
            (parts[0], 0), (parts[1], 0), (parts[0], 1), (parts[1], 1),
            (parts[2], 0), (parts[3], 0), (parts[2], 1), (parts[3], 1),
        ]
        for j, (part, tail) in enumerate(ends):
            extra = jnp.where(lane == 2 * j + s, lanes(part, 2 * j + s + tail), extra)

    quads = [edge_quads(from_left[h], from_right[h]) for h in range(2)]

    def rows(k, state):
        last, first, chain = state
        for n in range(8):
            row, pair = 8 * k + n, 4 * k + n // 2
            inv, pulled = kept_ref[row, INV], kept_ref[row, PULLED]
            west, east, centre = kept_ref[row, WEST], kept_ref[row, EAST], kept_ref[row, CENTRE]
            below, above = kept_ref[row, BELOW], kept_ref[row, ABOVE]
            new_last, new_first = [], []
            for h in range(2):
                q = c_ref[row, 8 * h : 8 * h + 8, :]
                left, right = neighbours(q, quads[h], (8 * k, n))
                tracer = 4 * (n % 2) + 2 * h
                source = jnp.where(
                    sub == 0,
                    em_ref[pair, tracer : tracer + 1, :],
                    jnp.where(sub == 4, em_ref[pair, tracer + 1 : tracer + 2, :], 0.0),
                )
                side = (centre * q + fluid * source) + (west * left + east * right)
                side = side + (below * subs(q, 1) + above * subs(q, -1))
                value = side * inv + pulled * last[h]
                side_ref[row, 8 * h : 8 * h + 8, :] = side
                partial_ref[row, 8 * h : 8 * h + 8, :] = value
                new_last.append(value)
                new_first.append(first[h] + chain * value)
            last, first = new_last, new_first
            chain = chain * (push * inv)
        return last, first, chain

    zero = jnp.zeros((SUB, LANE), jnp.float32)
    state = ([zero, zero], [zero, zero], zero + 1.0)
    last, first, _ = stepped(rows, state, PEEL)
    rows_ref[0], rows_ref[1] = first
    rows_ref[2], rows_ref[3] = last
    rows_ref[4] = ends_ref[0]
    rows_ref[5] = ends_ref[1]
    rows_ref[6] = extra


def blocks_of(rows_ref):
    main, extra = [], []
    for k in range(rows_ref.shape[0]):
        first_prev, first_next = both_rows(rows_ref[k, 4])
        last_prev, last_next = both_rows(rows_ref[k, 5])
        main.append(
            ([rows_ref[k, 0], rows_ref[k, 1]], [rows_ref[k, 2], rows_ref[k, 3]],
             first_prev, first_next, last_prev, last_next)
        )
        e = [lanes(rows_ref[k, 6], -2 * j) for j in range(8)]
        extra.append((e[0:2], e[2:4], e[4], e[5], e[6], e[7]))
    return main, extra


def joined(before, after):
    first, last, first_prev, first_next, last_prev, last_next = before
    first_b, last_b, first_prev_b, first_next_b, last_prev_b, last_next_b = after
    inv = 1.0 / (1.0 - last_next * first_prev_b)
    low_own = [(last[h] + last_next * first_b[h]) * inv for h in range(2)]
    low_prev, low_next = last_prev * inv, last_next * first_next_b * inv
    high_own = [first_b[h] + first_prev_b * low_own[h] for h in range(2)]
    high_prev, high_next = first_prev_b * low_prev, first_next_b + first_prev_b * low_next
    return (
        [first[h] + first_next * high_own[h] for h in range(2)],
        [last_b[h] + last_prev_b * low_own[h] for h in range(2)],
        first_prev + first_next * high_prev,
        first_next * high_next,
        last_prev_b * low_prev,
        last_next_b + last_prev_b * low_next,
    )


def condense_kernel(rows_ref, out_ref):
    main, extra = (functools.reduce(joined, forms) for forms in blocks_of(rows_ref))
    low, lane = sub_ids() < 4, lane_ids()
    out_ref[0], out_ref[1] = main[0]
    out_ref[2], out_ref[3] = main[1]
    out_ref[4] = jnp.where(low, main[2], main[3])
    out_ref[5] = jnp.where(low, main[4], main[5])
    packed = extra[0][0]
    for j, part in enumerate((extra[0][1], *extra[1], *extra[2:]), 1):
        packed = jnp.where(lane // 2 == j, lanes(part, 2 * j), packed)
    out_ref[6] = packed


def half_kernel(rows_ref, out_ref):
    main, extra = (functools.reduce(joined, forms) for forms in blocks_of(rows_ref))
    lane = lane_ids()
    lower = lax.axis_index("gx") < lax.axis_size("gx") // 2

    def facing(form):
        first, last, first_prev, _, _, last_next = form
        own = [jnp.where(lower, last[h], first[h]) for h in range(2)]
        return (*own, jnp.where(lower, last_next, first_prev))

    for n, part in enumerate(facing(main)):
        out_ref[n] = part
    parts = facing(extra)
    packed = parts[0]
    for j in (1, 2):
        packed = jnp.where(lane // 2 == j, lanes(parts[j], 2 * j), packed)
    out_ref[3] = packed


def halves(lower_side, upper_side, lower):
    last, last_next = lower_side[0:2], lower_side[2]
    first, first_prev = upper_side[0:2], upper_side[2]
    inv = 1.0 / (1.0 - last_next * first_prev)
    ends = [(last[h] + last_next * first[h]) * inv for h in range(2)]
    starts = [first[h] + first_prev * ends[h] for h in range(2)]
    return [jnp.where(lower, 0.0, ends[h]) for h in range(2)], [jnp.where(lower, starts[h], 0.0) for h in range(2)]


def interface(blocks, place, before, beyond):
    zero = jnp.zeros((SUB, LANE), jnp.float32)
    own, slope = before, zero
    kept_own, kept_slope = own, slope
    forms = []
    for k, (first, last, first_prev, first_next, last_prev, last_next) in enumerate(blocks):
        if k:
            here = place == k
            kept_own = [jnp.where(here, own[h], kept_own[h]) for h in range(2)]
            kept_slope = jnp.where(here, slope, kept_slope)
        inv = 1.0 / (1.0 - first_prev * slope)
        start = [(first[h] + first_prev * own[h]) * inv for h in range(2)]
        start_next = first_next * inv
        forms.append((start, start_next))
        carried = last_prev * slope
        own = [last[h] + last_prev * own[h] + carried * start[h] for h in range(2)]
        slope = last_next + carried * start_next
    after = beyond
    following, mine = after, after
    for k in reversed(range(len(forms))):
        following = [jnp.where(place == k, after[h], following[h]) for h in range(2)]
        start, start_next = forms[k]
        after = [start[h] + start_next * after[h] for h in range(2)]
        mine = [jnp.where(place == k, after[h], mine[h]) for h in range(2)]
    preceding = [kept_own[h] + kept_slope * mine[h] for h in range(2)]
    return preceding, following


def finish_kernel(
    side_ref, partial_ref, kept_ref, ghost_ref, near_ref, pair_ref, half_ref, building_ref, out_hbm, out_ref, sems
):
    push = cross_diff * fluid_of(building_ref)
    place = lax.axis_index("gx")
    quarter = near_ref.shape[0]
    lower = place < lax.axis_size("gx") // 2
    preceding, following = halves(*([half_ref[k, n] for n in range(3)] for k in range(2)), lower)
    ghost_prev, ghost_next = halves(*([lanes(half_ref[k, 3], -2 * n) for n in range(3)] for k in range(2)), lower)
    for ref, at in ((pair_ref, place // quarter % 2), (near_ref, place % quarter)):
        main, extra = blocks_of(ref)
        preceding, following = interface(main, at, preceding, following)
        ghost_prev, ghost_next = interface(extra, at, ghost_prev, ghost_next)
    ghosts = []
    for s in range(2):
        ghosts.append(
            [
                ghost_ref[4 * s + h]
                + ghost_ref[4 * s + 2] * ghost_prev[h][:, s : s + 1]
                + ghost_ref[4 * s + 3] * ghost_next[h][:, s : s + 1]
                for h in range(2)
            ]
        )
    quads = [edge_quads(ghosts[0][h], ghosts[1][h]) for h in range(2)]

    def rows(step, after):
        k = 15 - step
        for n in reversed(range(8)):
            row = 8 * k + n
            ratio, from_prev = push * kept_ref[row, INV], kept_ref[row, FROM_PREV]
            west, east = kept_ref[row, WEST], kept_ref[row, EAST]
            near, near_low, near_up = kept_ref[row, NEAR], kept_ref[row, NEAR_LOW], kept_ref[row, NEAR_UP]
            far, far_low, far_up = kept_ref[row, FAR], kept_ref[row, FAR_LOW], kept_ref[row, FAR_UP]
            centre = 2.0 - west - east
            new_after = []
            for h in range(2):
                at = slice(8 * h, 8 * h + 8)
                star = (partial_ref[row, at, :] + from_prev * preceding[h]) + ratio * after[h]
                left, right = neighbours(star, quads[h], (8 * k, n))
                side = (centre * star - side_ref[row, at, :]) + (west * left + east * right)
                value = near * side + near_low * subs(side, 1) + near_up * subs(side, -1)
                out_ref[row, at, :] = far * value + far_low * subs(value, 2) + far_up * subs(value, -2)
                new_after.append(star)
            after = new_after
        written(k).start()
        return after

    def written(k):
        return pltpu.make_async_copy(out_ref.at[pl.ds(8 * k, 8)], out_hbm.at[pl.ds(8 * k, 8)], sems.at[k])

    stepped(rows, following, PEEL_FINISH)
    for k in range(16):
        written(k).wait()


def call(kernel, out_shapes, in_specs, flops, bytes_accessed, limit=LIMIT, scratch=(), out_space=VMEM):
    return pl.pallas_call(
        kernel,
        out_shape=[jax.ShapeDtypeStruct(shape, jnp.float32) for shape in out_shapes],
        in_specs=in_specs,
        out_specs=[out_space] * len(out_shapes),
        scratch_shapes=list(scratch),
        compiler_params=pltpu.CompilerParams(vmem_limit_bytes=limit),
        cost_estimate=pl.CostEstimate(flops=flops, bytes_accessed=bytes_accessed, transcendentals=0),
    )


def on_device(concentration, courant_x, courant_y, vert_diff, emission, building):
    cells, tracers, levels, span = concentration.shape
    blocks = lax.axis_size("gx")
    devices = lax.axis_size("gy")
    c = concentration.reshape(cells, tracers * levels, span)
    coefs = [x.reshape(cells // 2, 2 * levels, span) for x in (courant_x, courant_y, vert_diff, emission)]
    field = (cells, 2 * SUB, LANE)
    packed = (6, SUB, LANE)
    sent_a, sent_b, c, cx, cy, vd, em = call(
        pack_kernel,
        [packed, packed, field] + [x.shape for x in coefs],
        [HBM] * 5 + [SMEM],
        10**6,
        2 * 10**6,
        scratch=[pltpu.SemaphoreType.DMA((CHUNKS + 4,))],
    )(*(pltpu.with_memory_space_constraint(x, pltpu.HBM) for x in (c, *coefs)), building)
    half = devices // 4 * 2
    even = [(i, i + 1) for i in range(0, devices, 2)]
    odd = [(i, (i + 1) % devices) for i in range(1, devices, 2)]
    low, high = [p for p in even if p[0] < half], [p for p in even if p[0] >= half]
    got_early, got_b, got_late = (
        lax.ppermute(sent, "gy", pairs + [(b, a) for a, b in pairs])
        for sent, pairs in ((sent_a, low), (sent_b, odd), (sent_a, high))
    )
    kept, ends = call(
        factor_kernel, [(cells, KEPT, SUB, LANE), (2, SUB, LANE)], [VMEM] * 3 + [SMEM, ANY], 10**7, 10**7
    )(cx, cy, vd, building, got_early)
    side, partial, ghost, mine = call(
        side_kernel, [field, field, (8, SUB, LANE), (7, SUB, LANE)], [VMEM] * 4 + [SMEM] + [VMEM] * 5, 10**7, 10**7
    )(c, em, kept, ends, building, sent_a, sent_b, got_early, got_b, got_late)
    quarter = blocks // 4
    near_groups = [[q * quarter + i for i in range(quarter)] for q in range(4)]
    pair_groups = [[q * quarter + i, (q + 1) * quarter + (i + quarter // 2) % quarter] for q in (0, 2) for i in range(quarter)]
    half_groups = [[q * quarter + i, r * quarter + (i + quarter // 2) % quarter] for q, r in ((1, 2), (0, 3)) for i in range(quarter)]
    near = lax.all_gather(mine, "gx", axis_index_groups=near_groups)
    (mine,) = call(condense_kernel, [mine.shape], [VMEM], 10**5, 10**5)(near)
    pair = lax.all_gather(mine, "gx", axis_index_groups=pair_groups)
    (mine,) = call(half_kernel, [(4, SUB, LANE)], [VMEM], 10**5, 10**5)(pair)
    half = lax.all_gather(mine, "gx", axis_index_groups=half_groups)
    (updated,) = call(
        finish_kernel,
        [field],
        [VMEM] * 7 + [SMEM],
        10**7,
        10**7,
        scratch=[pltpu.VMEM(field, jnp.float32), pltpu.SemaphoreType.DMA((16,))],
        out_space=HBM,
    )(side, partial, kept, ghost, near, pair, half, building)
    return updated.reshape(concentration.shape)


def solution(mesh):
    in_specs = (
        P("gx", None, None, "gy"),
        P("gx", None, "gy"),
        P("gx", None, "gy"),
        P("gx", None, "gy"),
        P("gx", None, "gy"),
        P("gx", "gy"),
    )
    return jax.shard_map(
        on_device, mesh=mesh, in_specs=in_specs, out_specs=P("gx", None, None, "gy"), check_vma=False
    )
```

```python
import functools

import jax
import jax.numpy as jnp
from jax import lax
from jax.experimental import pallas as pl
from jax.experimental.pallas import tpu as pltpu
from jax.sharding import PartitionSpec as P

cross_diff = 300.0
span_diff = 0.25

SUB, LANE = 8, 128
VMEM = pl.BlockSpec(memory_space=pltpu.VMEM)
HBM = pl.BlockSpec(memory_space=pltpu.HBM)
ANY = pl.BlockSpec(memory_space=pl.ANY)
SMEM = pl.BlockSpec(memory_space=pltpu.SMEM)
LIMIT = 16 * 1024 * 1024
(INV, PULLED, FROM_PREV, WEST, EAST, CENTRE, BELOW, ABOVE, NEAR, NEAR_LOW, NEAR_UP, FAR, FAR_LOW, FAR_UP) = range(14)
KEPT = 14
CHUNKS = 1
PEEL = 16
PEEL_FACTOR = 16
PEEL_FINISH = 16


def sub_ids():
    return lax.broadcasted_iota(jnp.int32, (SUB, LANE), 0)


def lane_ids():
    return lax.broadcasted_iota(jnp.int32, (SUB, LANE), 1)


def lanes(x, shift):
    shift %= LANE
    return pltpu.roll(x, shift, 1) if shift else x


def subs(x, shift):
    shift %= SUB
    return pltpu.roll(x, shift, 0) if shift else x


def stepped(body, state, peeled):
    for k in range(peeled):
        state = body(k, state)
    return lax.fori_loop(peeled, 16, body, state) if peeled < 16 else state


def fluid_of(building_ref):
    return 1.0 - building_ref[0, 0].astype(jnp.float32)


def both_rows(pair):
    low = sub_ids() < 4
    turned = subs(pair, 4)
    return jnp.where(low, pair, turned), jnp.where(low, turned, pair)


def level_above(x):
    return jnp.where(sub_ids() % 4 == 3, 0.0, subs(x, -1))


def level_below(x):
    return jnp.where(sub_ids() % 4 == 0, 0.0, subs(x, 1))


def edge_quads(west, east):
    at_west = lane_ids() % 4 == 2
    return [jnp.where(at_west, lanes(west, 2 - g), lanes(east, 1 - g)) for g in range(4)]


def neighbours(q, quads, row):
    base, offset = row
    turn = 126 - base - offset // 4 * 4
    edge = pltpu.roll(quads[offset % 4], turn, 1)
    lane = lane_ids()
    return jnp.where(lane == 0, edge, lanes(q, 1)), jnp.where(lane == LANE - 1, edge, lanes(q, -1))


def pack_kernel(
    c_hbm, cx_hbm, cy_hbm, vd_hbm, em_hbm, building_ref,
    a_ref, b_ref, c_ref, cx_ref, cy_ref, vd_ref, em_ref, sems,
):
    coefs = ((cx_hbm, cx_ref), (cy_hbm, cy_ref), (vd_hbm, vd_ref), (em_hbm, em_ref))
    size = c_ref.shape[0] // CHUNKS
    copies = [
        pltpu.make_async_copy(c_hbm.at[pl.ds(n * size, size)], c_ref.at[pl.ds(n * size, size)], sems.at[n])
        for n in range(CHUNKS)
    ]
    copies += [pltpu.make_async_copy(src, dst, sems.at[CHUNKS + n]) for n, (src, dst) in enumerate(coefs)]
    for copy in copies[CHUNKS:] + copies[:CHUNKS]:
        copy.start()

    lane, sub = lane_ids(), sub_ids()
    fluid = fluid_of(building_ref)
    low = sub < 4
    even_gy = lax.rem(lax.axis_index("gy"), 2) == 0
    quarter = lane // 4
    zero = jnp.zeros((SUB, LANE), jnp.float32)
    even = lane % 2 == 0
    pair_of = lane // 2
    first, last = [], []
    for n, (_, ref) in enumerate(coefs):
        copies[CHUNKS + n].wait()
        acc = zero
        for k in range(64):
            acc = jnp.where(pair_of == k, lanes(ref[k], 2 * k + 1), acc)
        turned = subs(acc, 4)
        at_even = jnp.where(low, acc, turned)
        at_odd = jnp.where(low, turned, acc)
        last.append(jnp.where(even, at_even, lanes(at_odd, 1)))
        first.append(jnp.where(even, lanes(at_even, -1), at_odd))
    picked = [[zero] * 4 for _ in range(2)]
    for n in range(CHUNKS):
        copies[n].wait()
        for m in range(n * size // 4, (n + 1) * size // 4):
            here = quarter == m
            for g in range(4):
                for half in range(2):
                    turned = lanes(c_ref[4 * m + g, 8 * half : 8 * half + 8, :], 4 * m + 2)
                    picked[half][g] = jnp.where(here, turned, picked[half][g])
    columns = []
    for half in range(2):
        found = []
        for j in range(4):
            out = lanes(picked[half][0], -j)
            for g in range(1, 4):
                out = jnp.where(lane % 4 == g, lanes(picked[half][g], g - j), out)
            found.append(out)
        columns.append(found)
    sides = []
    for (outer, inner), edge in (((2, 3), first), ((1, 0), last)):
        pull = fluid * (edge[0] + cross_diff)
        sides.append(
            [
                columns[0][outer],
                columns[1][outer],
                columns[0][inner],
                columns[1][inner],
                jnp.where(low, pull, edge[1]),
                jnp.where(low, edge[2], edge[3]),
            ]
        )
    for n in range(6):
        to_left, to_right = sides[0][n], sides[1][n]
        a_ref[n] = jnp.where(even_gy, to_right, to_left)
        b_ref[n] = jnp.where(even_gy, to_left, to_right)


def factor_kernel(cx_ref, cy_ref, vd_ref, building_ref, early_ref, kept_ref, ends_ref):
    fluid = fluid_of(building_ref)
    push = cross_diff * fluid
    ground = sub_ids() % 4 == 0

    def rows(k, state):
        ratio, from_prev, chain, first_prev = state
        for u in range(4):
            pair = 4 * k + u
            wind, face = cy_ref[pair], vd_ref[pair]
            face_up = level_above(face)
            west = fluid * (jnp.maximum(wind, 0.0) + span_diff)
            east = fluid * (jnp.maximum(-wind, 0.0) + span_diff)
            inv = 1.0 / (1.0 + face + face_up)
            lower = jnp.where(ground, 0.0, face * inv)
            upper = face_up * inv
            near = 1.0 / (1.0 - lower * subs(upper, 1) - upper * subs(lower, -1))
            near_low, near_up = near * lower, near * upper
            far_low, far_up = near_low * subs(lower, 1), near_up * subs(upper, -1)
            far = 1.0 / (1.0 - far_low * subs(far_up, 2) - far_up * subs(far_low, -2))
            scale = fluid * inv
            pairs = {
                WEST: west,
                EAST: east,
                CENTRE: fluid * (1.0 - face - face_up) - west - east,
                BELOW: jnp.where(ground, 0.0, fluid * face),
                ABOVE: fluid * face_up,
                NEAR: near * scale,
                NEAR_LOW: near_low * subs(scale, 1),
                NEAR_UP: near_up * subs(scale, -1),
                FAR: far,
                FAR_LOW: far * far_low,
                FAR_UP: far * far_up,
            }
            for n, value in pairs.items():
                kept_ref[2 * pair, n], kept_ref[2 * pair + 1, n] = both_rows(value)
            for r, pull in enumerate(both_rows(fluid * (cx_ref[pair] + cross_diff))):
                row = 2 * pair + r
                inv = 1.0 / ((1.0 + pull + push) - pull * ratio)
                pulled = pull * inv
                from_prev = pulled * from_prev
                first_prev = first_prev + chain * from_prev
                ratio = push * inv
                chain = chain * ratio
                kept_ref[row, INV] = inv
                kept_ref[row, PULLED] = pulled
                kept_ref[row, FROM_PREV] = from_prev
        return ratio, from_prev, chain, first_prev

    zero = jnp.zeros((SUB, LANE), jnp.float32)
    ratio, from_prev, chain, first_prev = stepped(
        rows, (zero, zero + 1.0, zero + 1.0, zero), PEEL_FACTOR
    )
    low = sub_ids() < 4
    ends_ref[0] = jnp.where(low, first_prev, chain)
    ends_ref[1] = jnp.where(low, from_prev, ratio)


def merge(left, right, part):
    low = sub_ids() < 4
    return jnp.where(low, left, subs(right, 4)) if part == 0 else jnp.where(low, subs(left, 4), right)


def ghost_columns(from_left, from_right, own_left, own_right):
    lane, sub = lane_ids(), sub_ids()
    pull, wind = merge(from_left[4], from_right[4], 0), merge(from_left[4], from_right[4], 1)
    face, emitted = merge(from_left[5], from_right[5], 0), merge(from_left[5], from_right[5], 1)
    fluid = jnp.where(pull > 0.0, 1.0, 0.0)
    face_up = level_above(face)
    west = jnp.maximum(wind, 0.0) + span_diff
    east = jnp.maximum(-wind, 0.0) + span_diff
    inv = 1.0 / (1.0 + pull + cross_diff * fluid)
    lower = pull * inv
    upper = cross_diff * fluid * inv
    sides = []
    for t in range(4):
        h, part = t // 2, t % 2
        q = merge(from_left[h], from_right[h], part)
        left = merge(from_left[2 + h], own_right[h], part)
        right = merge(own_left[h], from_right[2 + h], part)
        side = q + west * (left - q) + east * (right - q)
        side = side + face * (level_below(q) - q) + face_up * (level_above(q) - q)
        side = side + jnp.where(sub % 4 == 0, subs(emitted, -t), 0.0)
        sides.append(inv * fluid * side)
    sides.append(jnp.where(lane == 0, lower, 0.0))
    sides.append(jnp.where(lane == LANE - 1, upper, 0.0))
    lower = jnp.where(lane == 0, 0.0, lower)
    upper = jnp.where(lane == LANE - 1, 0.0, upper)
    step = 1
    while step < LANE:
        low_prev, up_prev = lanes(lower, step), lanes(upper, step)
        low_next, up_next = lanes(lower, -step), lanes(upper, -step)
        inv = 1.0 / (1.0 - lower * up_prev - upper * low_next)
        from_low, from_up = inv * lower, inv * upper
        sides = [inv * s + from_low * lanes(s, step) + from_up * lanes(s, -step) for s in sides]
        lower, upper = from_low * low_prev, from_up * up_next
        step *= 2
    prev, following = both_rows(sides[4]), both_rows(sides[5])
    return [
        [merge(sides[0], sides[1], s), merge(sides[2], sides[3], s), prev[s], following[s]] for s in range(2)
    ]


def side_kernel(
    c_ref, em_ref, kept_ref, ends_ref, building_ref, sent_a_ref, sent_b_ref, got_early_ref, got_b_ref, got_late_ref,
    side_ref, partial_ref, ghost_ref, rows_ref,
):
    lane, sub = lane_ids(), sub_ids()
    fluid = fluid_of(building_ref)
    push = cross_diff * fluid
    even_gy = lax.rem(lax.axis_index("gy"), 2) == 0
    own_left = [jnp.where(even_gy, sent_b_ref[n], sent_a_ref[n]) for n in range(2)]
    own_right = [jnp.where(even_gy, sent_a_ref[n], sent_b_ref[n]) for n in range(2)]
    early = lax.axis_index("gy") < lax.axis_size("gy") // 4 * 2
    got_a = [jnp.where(early, got_early_ref[n], got_late_ref[n]) for n in range(6)]
    from_left = [jnp.where(even_gy, got_b_ref[n], got_a[n]) for n in range(6)]
    from_right = [jnp.where(even_gy, got_a[n], got_b_ref[n]) for n in range(6)]

    extra = jnp.zeros((SUB, LANE), jnp.float32)
    for s, parts in enumerate(ghost_columns(from_left, from_right, own_left, own_right)):
        for n in range(4):
            ghost_ref[4 * s + n] = parts[n]
        ends = [
            (parts[0], 0), (parts[1], 0), (parts[0], 1), (parts[1], 1),
            (parts[2], 0), (parts[3], 0), (parts[2], 1), (parts[3], 1),
        ]
        for j, (part, tail) in enumerate(ends):
            extra = jnp.where(lane == 2 * j + s, lanes(part, 2 * j + s + tail), extra)

    quads = [edge_quads(from_left[h], from_right[h]) for h in range(2)]

    def rows(k, state):
        last, first, chain = state
        for n in range(8):
            row, pair = 8 * k + n, 4 * k + n // 2
            inv, pulled = kept_ref[row, INV], kept_ref[row, PULLED]
            west, east, centre = kept_ref[row, WEST], kept_ref[row, EAST], kept_ref[row, CENTRE]
            below, above = kept_ref[row, BELOW], kept_ref[row, ABOVE]
            new_last, new_first = [], []
            for h in range(2):
                q = c_ref[row, 8 * h : 8 * h + 8, :]
                left, right = neighbours(q, quads[h], (8 * k, n))
                tracer = 4 * (n % 2) + 2 * h
                source = jnp.where(
                    sub == 0,
                    em_ref[pair, tracer : tracer + 1, :],
                    jnp.where(sub == 4, em_ref[pair, tracer + 1 : tracer + 2, :], 0.0),
                )
                side = (centre * q + fluid * source) + (west * left + east * right)
                side = side + (below * subs(q, 1) + above * subs(q, -1))
                value = side * inv + pulled * last[h]
                side_ref[row, 8 * h : 8 * h + 8, :] = side
                partial_ref[row, 8 * h : 8 * h + 8, :] = value
                new_last.append(value)
                new_first.append(first[h] + chain * value)
            last, first = new_last, new_first
            chain = chain * (push * inv)
        return last, first, chain

    zero = jnp.zeros((SUB, LANE), jnp.float32)
    state = ([zero, zero], [zero, zero], zero + 1.0)
    last, first, _ = stepped(rows, state, PEEL)
    rows_ref[0], rows_ref[1] = first
    rows_ref[2], rows_ref[3] = last
    rows_ref[4] = ends_ref[0]
    rows_ref[5] = ends_ref[1]
    rows_ref[6] = extra


def blocks_of(rows_ref):
    main, extra = [], []
    for k in range(rows_ref.shape[0]):
        first_prev, first_next = both_rows(rows_ref[k, 4])
        last_prev, last_next = both_rows(rows_ref[k, 5])
        main.append(
            ([rows_ref[k, 0], rows_ref[k, 1]], [rows_ref[k, 2], rows_ref[k, 3]],
             first_prev, first_next, last_prev, last_next)
        )
        e = [lanes(rows_ref[k, 6], -2 * j) for j in range(8)]
        extra.append((e[0:2], e[2:4], e[4], e[5], e[6], e[7]))
    return main, extra


def joined(before, after):
    first, last, first_prev, first_next, last_prev, last_next = before
    first_b, last_b, first_prev_b, first_next_b, last_prev_b, last_next_b = after
    inv = 1.0 / (1.0 - last_next * first_prev_b)
    low_own = [(last[h] + last_next * first_b[h]) * inv for h in range(2)]
    low_prev, low_next = last_prev * inv, last_next * first_next_b * inv
    high_own = [first_b[h] + first_prev_b * low_own[h] for h in range(2)]
    high_prev, high_next = first_prev_b * low_prev, first_next_b + first_prev_b * low_next
    return (
        [first[h] + first_next * high_own[h] for h in range(2)],
        [last_b[h] + last_prev_b * low_own[h] for h in range(2)],
        first_prev + first_next * high_prev,
        first_next * high_next,
        last_prev_b * low_prev,
        last_next_b + last_prev_b * low_next,
    )


def condense_kernel(rows_ref, out_ref):
    main, extra = (functools.reduce(joined, forms) for forms in blocks_of(rows_ref))
    low, lane = sub_ids() < 4, lane_ids()
    out_ref[0], out_ref[1] = main[0]
    out_ref[2], out_ref[3] = main[1]
    out_ref[4] = jnp.where(low, main[2], main[3])
    out_ref[5] = jnp.where(low, main[4], main[5])
    packed = extra[0][0]
    for j, part in enumerate((extra[0][1], *extra[1], *extra[2:]), 1):
        packed = jnp.where(lane // 2 == j, lanes(part, 2 * j), packed)
    out_ref[6] = packed


def half_kernel(rows_ref, out_ref):
    main, extra = (functools.reduce(joined, forms) for forms in blocks_of(rows_ref))
    lane = lane_ids()
    lower = lax.axis_index("gx") < lax.axis_size("gx") // 2

    def facing(form):
        first, last, first_prev, _, _, last_next = form
        own = [jnp.where(lower, last[h], first[h]) for h in range(2)]
        return (*own, jnp.where(lower, last_next, first_prev))

    for n, part in enumerate(facing(main)):
        out_ref[n] = part
    parts = facing(extra)
    packed = parts[0]
    for j in (1, 2):
        packed = jnp.where(lane // 2 == j, lanes(parts[j], 2 * j), packed)
    out_ref[3] = packed


def halves(lower_side, upper_side, lower):
    last, last_next = lower_side[0:2], lower_side[2]
    first, first_prev = upper_side[0:2], upper_side[2]
    inv = 1.0 / (1.0 - last_next * first_prev)
    ends = [(last[h] + last_next * first[h]) * inv for h in range(2)]
    starts = [first[h] + first_prev * ends[h] for h in range(2)]
    return [jnp.where(lower, 0.0, ends[h]) for h in range(2)], [jnp.where(lower, starts[h], 0.0) for h in range(2)]


def interface(blocks, place, before, beyond):
    zero = jnp.zeros((SUB, LANE), jnp.float32)
    own, slope = before, zero
    kept_own, kept_slope = own, slope
    forms = []
    for k, (first, last, first_prev, first_next, last_prev, last_next) in enumerate(blocks):
        if k:
            here = place == k
            kept_own = [jnp.where(here, own[h], kept_own[h]) for h in range(2)]
            kept_slope = jnp.where(here, slope, kept_slope)
        inv = 1.0 / (1.0 - first_prev * slope)
        start = [(first[h] + first_prev * own[h]) * inv for h in range(2)]
        start_next = first_next * inv
        forms.append((start, start_next))
        carried = last_prev * slope
        own = [last[h] + last_prev * own[h] + carried * start[h] for h in range(2)]
        slope = last_next + carried * start_next
    after = beyond
    following, mine = after, after
    for k in reversed(range(len(forms))):
        following = [jnp.where(place == k, after[h], following[h]) for h in range(2)]
        start, start_next = forms[k]
        after = [start[h] + start_next * after[h] for h in range(2)]
        mine = [jnp.where(place == k, after[h], mine[h]) for h in range(2)]
    preceding = [kept_own[h] + kept_slope * mine[h] for h in range(2)]
    return preceding, following


def finish_kernel(
    side_ref, partial_ref, kept_ref, ghost_ref, near_ref, pair_ref, half_ref, building_ref, out_hbm, out_ref, sems
):
    push = cross_diff * fluid_of(building_ref)
    place = lax.axis_index("gx")
    quarter = near_ref.shape[0]
    lower = place < lax.axis_size("gx") // 2
    preceding, following = halves(*([half_ref[k, n] for n in range(3)] for k in range(2)), lower)
    ghost_prev, ghost_next = halves(*([lanes(half_ref[k, 3], -2 * n) for n in range(3)] for k in range(2)), lower)
    for ref, at in ((pair_ref, place // quarter % 2), (near_ref, place % quarter)):
        main, extra = blocks_of(ref)
        preceding, following = interface(main, at, preceding, following)
        ghost_prev, ghost_next = interface(extra, at, ghost_prev, ghost_next)
    ghosts = []
    for s in range(2):
        ghosts.append(
            [
                ghost_ref[4 * s + h]
                + ghost_ref[4 * s + 2] * ghost_prev[h][:, s : s + 1]
                + ghost_ref[4 * s + 3] * ghost_next[h][:, s : s + 1]
                for h in range(2)
            ]
        )
    quads = [edge_quads(ghosts[0][h], ghosts[1][h]) for h in range(2)]

    def rows(step, after):
        k = 15 - step
        for n in reversed(range(8)):
            row = 8 * k + n
            ratio, from_prev = push * kept_ref[row, INV], kept_ref[row, FROM_PREV]
            west, east = kept_ref[row, WEST], kept_ref[row, EAST]
            near, near_low, near_up = kept_ref[row, NEAR], kept_ref[row, NEAR_LOW], kept_ref[row, NEAR_UP]
            far, far_low, far_up = kept_ref[row, FAR], kept_ref[row, FAR_LOW], kept_ref[row, FAR_UP]
            centre = 2.0 - west - east
            new_after = []
            for h in range(2):
                at = slice(8 * h, 8 * h + 8)
                star = (partial_ref[row, at, :] + from_prev * preceding[h]) + ratio * after[h]
                left, right = neighbours(star, quads[h], (8 * k, n))
                side = (centre * star - side_ref[row, at, :]) + (west * left + east * right)
                value = near * side + near_low * subs(side, 1) + near_up * subs(side, -1)
                out_ref[row, at, :] = far * value + far_low * subs(value, 2) + far_up * subs(value, -2)
                new_after.append(star)
            after = new_after
        if k % 2 == 0:
            written(k // 2).start()
        return after

    def written(k):
        return pltpu.make_async_copy(out_ref.at[pl.ds(16 * k, 16)], out_hbm.at[pl.ds(16 * k, 16)], sems.at[k])

    stepped(rows, following, PEEL_FINISH)
    for k in range(8):
        written(k).wait()


def call(kernel, out_shapes, in_specs, flops, bytes_accessed, limit=LIMIT, scratch=(), out_space=VMEM):
    return pl.pallas_call(
        kernel,
        out_shape=[jax.ShapeDtypeStruct(shape, jnp.float32) for shape in out_shapes],
        in_specs=in_specs,
        out_specs=[out_space] * len(out_shapes),
        scratch_shapes=list(scratch),
        compiler_params=pltpu.CompilerParams(vmem_limit_bytes=limit),
        cost_estimate=pl.CostEstimate(flops=flops, bytes_accessed=bytes_accessed, transcendentals=0),
    )


def on_device(concentration, courant_x, courant_y, vert_diff, emission, building):
    cells, tracers, levels, span = concentration.shape
    blocks = lax.axis_size("gx")
    devices = lax.axis_size("gy")
    c = concentration.reshape(cells, tracers * levels, span)
    coefs = [x.reshape(cells // 2, 2 * levels, span) for x in (courant_x, courant_y, vert_diff, emission)]
    field = (cells, 2 * SUB, LANE)
    packed = (6, SUB, LANE)
    sent_a, sent_b, c, cx, cy, vd, em = call(
        pack_kernel,
        [packed, packed, field] + [x.shape for x in coefs],
        [HBM] * 5 + [SMEM],
        10**6,
        2 * 10**6,
        scratch=[pltpu.SemaphoreType.DMA((CHUNKS + 4,))],
    )(*(pltpu.with_memory_space_constraint(x, pltpu.HBM) for x in (c, *coefs)), building)
    half = devices // 4 * 2
    even = [(i, i + 1) for i in range(0, devices, 2)]
    odd = [(i, (i + 1) % devices) for i in range(1, devices, 2)]
    low, high = [p for p in even if p[0] < half], [p for p in even if p[0] >= half]
    got_early, got_b, got_late = (
        lax.ppermute(sent, "gy", pairs + [(b, a) for a, b in pairs])
        for sent, pairs in ((sent_a, low), (sent_b, odd), (sent_a, high))
    )
    kept, ends = call(
        factor_kernel, [(cells, KEPT, SUB, LANE), (2, SUB, LANE)], [VMEM] * 3 + [SMEM, ANY], 10**7, 10**7
    )(cx, cy, vd, building, got_early)
    side, partial, ghost, mine = call(
        side_kernel, [field, field, (8, SUB, LANE), (7, SUB, LANE)], [VMEM] * 4 + [SMEM] + [VMEM] * 5, 10**7, 10**7
    )(c, em, kept, ends, building, sent_a, sent_b, got_early, got_b, got_late)
    quarter = blocks // 4
    near_groups = [[q * quarter + i for i in range(quarter)] for q in range(4)]
    pair_groups = [[q * quarter + i, (q + 1) * quarter + (i + quarter // 2) % quarter] for q in (0, 2) for i in range(quarter)]
    half_groups = [[q * quarter + i, r * quarter + (i + quarter // 2) % quarter] for q, r in ((1, 2), (0, 3)) for i in range(quarter)]
    near = lax.all_gather(mine, "gx", axis_index_groups=near_groups)
    (mine,) = call(condense_kernel, [mine.shape], [VMEM], 10**5, 10**5)(near)
    pair = lax.all_gather(mine, "gx", axis_index_groups=pair_groups)
    (mine,) = call(half_kernel, [(4, SUB, LANE)], [VMEM], 10**5, 10**5)(pair)
    half = lax.all_gather(mine, "gx", axis_index_groups=half_groups)
    (updated,) = call(
        finish_kernel,
        [field],
        [VMEM] * 7 + [SMEM],
        10**7,
        10**7,
        scratch=[pltpu.VMEM(field, jnp.float32), pltpu.SemaphoreType.DMA((8,))],
        out_space=HBM,
    )(side, partial, kept, ghost, near, pair, half, building)
    return updated.reshape(concentration.shape)


def solution(mesh):
    in_specs = (
        P("gx", None, None, "gy"),
        P("gx", None, "gy"),
        P("gx", None, "gy"),
        P("gx", None, "gy"),
        P("gx", None, "gy"),
        P("gx", "gy"),
    )
    return jax.shard_map(
        on_device, mesh=mesh, in_specs=in_specs, out_specs=P("gx", None, None, "gy"), check_vma=False
    )
```
